256 devices in a mesh: src: 8 (over x, core), tgt: 32 (over z, y).
Axes of the slice: x: 4, y: 4, z: 8, core: 2. Of those that a mesh axis runs over, the one named last changes fastest.
Arguments:
- src_points: float32 [16, 65536], P(None, 'src'), may hold values from -24 to 24
- tgt_points: float32 [16, 32768], P(None, 'tgt'), may hold values from -24 to 24
- log_a: float32 [65536], P('src'), may hold values from -1 to 1
- log_b: float32 [32768], P('tgt'), may hold values from -1 to 1
- g_init: float32 [32768], P('tgt'), may hold values from -12 to 12
Outputs:
- f_new: float32 [65536], P('src')
- g_new: float32 [32768], P('tgt')
- src_map: float32 [16, 65536], P(None, ('src', 'tgt'))
- tgt_map: float32 [16, 32768], P(None, 'tgt')
The draws below stay inside these ranges and needn't reach their ends.
All inputs are finite; a program needn't handle non-finite values.
Results may differ from the reference program's by a relative error of at most 0.0003.
Values sent between devices are 32-bit elements; how exact they have to be, the bound alone decides.
No kernel may reach another device: no remote copies, remote signals or barrier semaphores. Data moves between devices by JAX's collectives and lax.ppermute only.
A program may use at most 128 MiB of HBM per device.

```python
import math
import jax
import jax.numpy as jnp
from jax import lax

DIM = 16
NS = 65536
NT = 32768


def draw_src_points(key, part):
    key = jax.random.fold_in(key, 1)
    return jnp.clip(jax.random.normal(key, (DIM, NS), jnp.float32), -5.0, 5.0)


def draw_tgt_points(key, part):
    key = jax.random.fold_in(key, 2)
    spacing = NT // 16
    positions = jnp.arange(NT)
    anchor_slot = positions // spacing % 16
    within = positions % spacing
    isolated = ((anchor_slot == 15) & (within == 1))[None, :]
    points = jnp.clip(jax.random.normal(key, (DIM, NT), jnp.float32), -5.0, 5.0)
    return jnp.where(isolated, 8.0, points)


def block_levels(stream_key, shape, cuts, smallest, top_value):
    def one(axis_at, blocks):
        draws = jax.random.uniform(jax.random.fold_in(jax.random.fold_in(stream_key, 6), axis_at), (blocks,), jnp.float32, smallest / len(cuts), top_value / len(cuts))
        return jnp.repeat(jnp.exp(draws), shape[axis_at] // blocks).reshape((-1,) + (1,) * (len(shape) - axis_at - 1))

    factor_of = one(*cuts[0])
    for cut in cuts[1:]:
        factor_of = factor_of * one(*cut)
    return factor_of


def noise(own_key, shape, width, reach, cuts=(), dtype=jnp.bfloat16):
    entries = jax.random.normal(own_key, shape, jnp.float32) * width
    if len(cuts) > 0:
        entries = block_levels(own_key, shape, cuts, -0.22, 0.18) * entries
    return jnp.clip(entries, min=-reach, max=reach).astype(dtype)


def setup_inputs(seed: int = 0) -> dict:
    arg_keys = jax.random.split(jax.random.key(seed), 6)
    return {
        "src_points": draw_src_points(jax.random.fold_in(arg_keys[5], 71), 0),
        "tgt_points": draw_tgt_points(jax.random.fold_in(arg_keys[5], 71), 0),
        "log_a": jnp.clip(jax.random.uniform(arg_keys[2], (NS,), jnp.float32, -1.0, 1.0) * block_levels(arg_keys[2], (NS,), ((0, 8),), -0.4, 0.0), -1.0, 1.0),
        "log_b": jnp.clip(jax.random.uniform(arg_keys[3], (NT,), jnp.float32, -1.0, 1.0) * block_levels(arg_keys[3], (NT,), ((0, 32),), -0.4, 0.0), -1.0, 1.0),
        "g_init": noise(arg_keys[4], (NT,), 2.0, 12.0, ((0, 32),), jnp.float32),
    }


entropy = 4.0
highest = lax.Precision.HIGHEST


def cost_tile(sources, targets):
    crossed = lax.dot_general(sources, targets, (((0,), (0,)), ((), ())), precision=highest, preferred_element_type=jnp.float32)
    return jnp.sum(sources * sources, 0)[:, None] + jnp.sum(targets * targets, 0)[None, :] - 2.0 * crossed


def split_rows(points, stride):
    blocks = points.shape[1] // stride
    return points.reshape(points.shape[0], blocks, stride).transpose(1, 0, 2)


def reference(src_points, tgt_points, log_a, log_b, g_init):
    stride = math.gcd(src_points.shape[1], 1024)
    pieces = split_rows(src_points, stride)

    def row_lse(sources):
        scores = (g_init[None, :] - cost_tile(sources, tgt_points)) / entropy
        row_peak = jnp.max(scores, 1)
        return row_peak + jnp.log(jnp.sum(jnp.exp(scores - row_peak[:, None]), 1))

    f_new = entropy * (log_a - lax.map(row_lse, pieces).reshape(-1))
    f_pieces = f_new.reshape(-1, stride)

    def column_step(carry, inputs):
        col_peak, col_sum, col_mass = carry
        sources, f_block = inputs
        scores = (f_block[:, None] - cost_tile(sources, tgt_points)) / entropy
        new_peak = jnp.maximum(col_peak, jnp.max(scores, 0))
        factor = jnp.exp(col_peak - new_peak)
        weights = jnp.exp(scores - new_peak[None, :])
        col_sum = col_sum * factor + jnp.sum(weights, 0)
        col_mass = col_mass * factor[None, :] + jnp.dot(sources, weights, precision=highest, preferred_element_type=jnp.float32)
        return (new_peak, col_sum, col_mass), None

    columns = tgt_points.shape[1]
    initial = (jnp.full((columns,), -jnp.inf, jnp.float32), jnp.zeros((columns,), jnp.float32), jnp.zeros((DIM, columns), jnp.float32))
    finals, unused = lax.scan(column_step, initial, (pieces, f_pieces))
    col_peak, col_sum, col_mass = finals
    g_new = entropy * (log_b - col_peak - jnp.log(col_sum))
    tgt_map = col_mass / col_sum[None, :]

    def row_map(sources):
        scores = (g_new[None, :] - cost_tile(sources, tgt_points)) / entropy
        row_peak = jnp.max(scores, 1)
        weights = jnp.exp(scores - row_peak[:, None])
        row_mass = lax.dot_general(tgt_points, weights, (((1,), (1,)), ((), ())), precision=highest, preferred_element_type=jnp.float32)
        return row_mass / jnp.sum(weights, 1)[None, :]

    src_map = lax.map(row_map, pieces).transpose(1, 0, 2).reshape(DIM, -1)
    return f_new, g_new, src_map, tgt_map
```

```python
import functools
import math

import jax
import jax.numpy as jnp
from jax import lax
from jax.experimental import pallas as pl
from jax.experimental.pallas import tpu as pltpu
from jax.sharding import PartitionSpec as P

LOG2E = math.log2(math.e)
LN2 = math.log(2.0)
ENTROPY = 4.0
ALPHA = LOG2E / ENTROPY
ROWS = 1024
LANES = 256
DEPTH = 128
bf16 = jnp.bfloat16
f32 = jnp.float32


def split3(values):
    first = values.astype(bf16).astype(f32)
    rest = values - first
    second = rest.astype(bf16).astype(f32)
    third = (rest - second).astype(bf16).astype(f32)
    return first, second, third


def stack_terms(points, potential):
    n = points.shape[1]
    a, b, c = split3(points)
    u, v, w = split3(potential)
    row = lax.broadcasted_iota(jnp.int32, (16, n), 0)
    extra = jnp.where(row == 0, u, jnp.where(row == 1, v, jnp.where(row == 2, w, 0.0)))
    return jnp.concatenate([a, b, c, a, b, a, extra, jnp.zeros((16, n), f32)], 0)


def stack_plain(points):
    n = points.shape[1]
    a, b, c = (part.astype(bf16) for part in split3(points))
    ones = jnp.ones((16, n), bf16)
    return jnp.concatenate([a, a, a, b, b, c, ones, jnp.zeros((16, n), bf16)], 0)


def column_max(x_ref):
    peak = jnp.max(x_ref[0:128, :], axis=0, keepdims=True)
    for at in range(128, ROWS, 128):
        peak = jnp.maximum(peak, jnp.max(x_ref[at : at + 128, :], axis=0, keepdims=True))
    return peak


def lse_kernel(src_ref, tgt_ref, g_ref, out_ref, rows_ref, cols_ref, x0_ref, x1_ref):
    tgt = tgt_ref[...]
    term = ALPHA * (g_ref[...] - jnp.sum(tgt * tgt, axis=0, keepdims=True))
    rows_ref[...] = stack_terms(tgt, term).T.astype(bf16)
    cols_ref[...] = stack_plain(src_ref[...] * (2.0 * ALPHA))
    tiles = src_ref.shape[1] // LANES

    def product(tile, x_ref):
        at = pl.multiple_of(tile * LANES, LANES)
        x_ref[...] = jnp.dot(
            rows_ref[...], cols_ref[:, pl.ds(at, LANES)], preferred_element_type=f32
        )

    def reduce(tile, x_ref):
        at = pl.multiple_of(tile * LANES, LANES)
        peak = column_max(x_ref)
        total = jnp.zeros((8, LANES), f32)
        for i in range(0, ROWS, 8):
            total = total + jnp.exp2(x_ref[i : i + 8, :] - peak)
        out_ref[:, pl.ds(at, LANES)] = peak + jnp.log2(
            jnp.sum(total, axis=0, keepdims=True)
        )

    product(0, x0_ref)

    def body(pair, carry):
        tile = pair * 2
        product(tile + 1, x1_ref)
        reduce(tile, x0_ref)
        product(jnp.minimum(tile + 2, tiles - 1), x0_ref)
        reduce(tile + 1, x1_ref)
        return carry

    lax.fori_loop(0, tiles // 2, body, 0)


def weigh(x_ref, hi_ref, lo_ref, heavy, light):
    peak = column_max(x_ref)
    for at in range(0, ROWS, 128):
        weights = jnp.exp2(x_ref[at : at + 128, :] - peak)
        hi = weights.astype(bf16)
        hi_ref[at : at + 128, :] = hi
        lo_ref[at : at + 128, :] = (weights - hi.astype(f32)).astype(bf16)
    big = jnp.dot(heavy, hi_ref[...], preferred_element_type=f32)
    small = jnp.dot(light, lo_ref[...], preferred_element_type=f32)
    return peak, big[0:16] + big[32:48] + small[0:16], big[16:32] + small[16:32]


def two_parts(points):
    first = points.astype(bf16)
    second = (points - first.astype(f32)).astype(bf16)
    return jnp.concatenate([first, jnp.ones(points.shape, bf16), second], 0)


def column_kernel(
    src_ref, tgt_ref, term_ref, out_ref, rows_ref, cols_ref, both_ref, x0_ref, x1_ref, hi_ref, lo_ref
):
    blocks = src_ref.shape[1] // ROWS
    tiles = tgt_ref.shape[1] // LANES
    cols_ref[...] = stack_plain(tgt_ref[...] * (2.0 * ALPHA))

    def build(block, carry):
        at = pl.multiple_of(block * ROWS, ROWS)
        src = src_ref[:, pl.ds(at, ROWS)]
        rows_ref[pl.ds(at, ROWS), :] = stack_terms(src, term_ref[:, pl.ds(at, ROWS)]).T.astype(bf16)
        both_ref[:, pl.ds(at, ROWS)] = two_parts(src)
        return carry

    lax.fori_loop(0, blocks, build, 0)
    out_ref[0:8, :] = jnp.full((8, tgt_ref.shape[1]), -1e30, f32)
    out_ref[8:40, :] = jnp.zeros((32, tgt_ref.shape[1]), f32)
    slots = (x0_ref, x1_ref)

    def product(block, tile, x_ref):
        at = pl.multiple_of(block * ROWS, ROWS)
        x_ref[...] = jnp.dot(
            rows_ref[pl.ds(at, ROWS), :],
            cols_ref[:, tile * LANES : (tile + 1) * LANES],
            preferred_element_type=f32,
        )

    def accumulate(block, tile, x_ref):
        at = pl.multiple_of(block * ROWS, ROWS)
        both = both_ref[:, pl.ds(at, ROWS)]
        peak, mass, total = weigh(x_ref, hi_ref, lo_ref, both, both[0:32])
        here = slice(tile * LANES, (tile + 1) * LANES)
        before = out_ref[0:1, here]
        after = jnp.maximum(before, peak)
        old = jnp.exp2(before - after)
        new = jnp.exp2(peak - after)
        out_ref[0:1, here] = after
        out_ref[8:24, here] = out_ref[8:24, here] * old + mass * new
        out_ref[24:40, here] = out_ref[24:40, here] * old + total * new

    product(0, 0, slots[0])

    def body(block, carry):
        for tile in range(tiles):
            if tile + 1 < tiles:
                product(block, tile + 1, slots[(tile + 1) % 2])
            else:
                product(jnp.minimum(block + 1, blocks - 1), 0, slots[(tile + 1) % 2])
            accumulate(block, tile, slots[tile % 2])
        return carry

    lax.fori_loop(0, blocks, body, 0)


def map_kernel(
    src_ref, tgt_ref, term_ref, out_ref, rows_ref, cols_ref, x0_ref, x1_ref, hi_ref, lo_ref
):
    tgt = tgt_ref[...]
    rows_ref[...] = stack_terms(tgt, term_ref[...]).T.astype(bf16)
    cols_ref[...] = stack_plain(src_ref[...] * (2.0 * ALPHA))
    tiles = src_ref.shape[1] // LANES
    both = two_parts(tgt)

    def product(tile, x_ref):
        at = pl.multiple_of(tile * LANES, LANES)
        x_ref[...] = jnp.dot(
            rows_ref[...], cols_ref[:, pl.ds(at, LANES)], preferred_element_type=f32
        )

    def reduce(tile, x_ref):
        at = pl.multiple_of(tile * LANES, LANES)
        peak, mass, total = weigh(x_ref, hi_ref, lo_ref, both, both[0:32])
        row = lax.broadcasted_iota(jnp.int32, (8, LANES), 0)
        out_ref[0:8, pl.ds(at, LANES)] = jnp.where(row == 0, peak, total[0:8])
        out_ref[8:24, pl.ds(at, LANES)] = mass

    product(0, x0_ref)

    def body(pair, carry):
        tile = pair * 2
        product(tile + 1, x1_ref)
        reduce(tile, x0_ref)
        product(jnp.minimum(tile + 2, tiles - 1), x0_ref)
        reduce(tile + 1, x1_ref)
        return carry

    lax.fori_loop(0, tiles // 2, body, 0)


params = pltpu.CompilerParams(vmem_limit_bytes=48 * 1024 * 1024)
vmem = pl.BlockSpec(memory_space=pltpu.VMEM)
tile_f32 = pltpu.VMEM((ROWS, LANES), f32)
tile_bf16 = pltpu.VMEM((ROWS, LANES), bf16)


def row_lse(src, tgt, g):
    n, k = src.shape[1], tgt.shape[1]
    return pl.pallas_call(
        lse_kernel,
        out_shape=jax.ShapeDtypeStruct((1, n), f32),
        in_specs=[vmem] * 3,
        out_specs=vmem,
        scratch_shapes=[
            pltpu.VMEM((k, DEPTH), bf16),
            pltpu.VMEM((DEPTH, n), bf16),
            tile_f32,
            tile_f32,
        ],
        compiler_params=params,
        name="row_lse",
    )(src, tgt, g)


def column_sums(src, tgt, term):
    n, k = src.shape[1], tgt.shape[1]
    return pl.pallas_call(
        column_kernel,
        out_shape=jax.ShapeDtypeStruct((40, k), f32),
        in_specs=[vmem] * 3,
        out_specs=vmem,
        scratch_shapes=[
            pltpu.VMEM((n, DEPTH), bf16),
            pltpu.VMEM((DEPTH, k), bf16),
            pltpu.VMEM((48, n), bf16),
            tile_f32,
            tile_f32,
            tile_bf16,
            tile_bf16,
        ],
        compiler_params=params,
        name="column_sums",
    )(src, tgt, term)


def row_sums(src, tgt, term):
    n, k = src.shape[1], tgt.shape[1]
    return pl.pallas_call(
        map_kernel,
        out_shape=jax.ShapeDtypeStruct((24, n), f32),
        in_specs=[vmem] * 3,
        out_specs=vmem,
        scratch_shapes=[
            pltpu.VMEM((k, DEPTH), bf16),
            pltpu.VMEM((DEPTH, n), bf16),
            tile_f32,
            tile_f32,
            tile_bf16,
            tile_bf16,
        ],
        compiler_params=params,
        name="row_sums",
    )(src, tgt, term)


def swap(values, axis, bit):
    size = lax.axis_size(axis)
    return lax.ppermute(values, axis, [(i, i ^ bit) for i in range(size)])


def per_device(src_points, tgt_points, log_a, log_b, g_init):
    share = src_points.shape[1] // lax.axis_size("tgt")
    with jax.named_scope("row_lse"):
        level = row_lse(src_points, tgt_points, g_init[None, :])[0]
    with jax.named_scope("row_combine"):
        bit = 1
        while bit < lax.axis_size("tgt"):
            other = swap(level, "tgt", bit)
            level = jnp.maximum(level, other) + jnp.log2(
                1.0 + jnp.exp2(-jnp.abs(level - other))
            )
            bit *= 2
        src_term = LOG2E * log_a - level
        f_new = ENTROPY * LN2 * src_term + jnp.sum(src_points * src_points, 0)

    with jax.named_scope("column_sums"):
        columns = column_sums(src_points, tgt_points, src_term[None, :])
        peak, sums = columns[0:1], columns[8:25]
    with jax.named_scope("column_combine"):
        bit = 1
        while bit < lax.axis_size("src"):
            theirs = swap(jnp.concatenate([peak, sums], 0), "src", bit)
            top = jnp.maximum(peak, theirs[0:1])
            sums = sums * jnp.exp2(peak - top) + theirs[1:] * jnp.exp2(theirs[0:1] - top)
            peak = top
            bit *= 2
        col_sum = sums[16]
        tgt_term = LOG2E * log_b - peak[0] - jnp.log2(col_sum)
        g_new = ENTROPY * LN2 * tgt_term + jnp.sum(tgt_points * tgt_points, 0)
        tgt_map = sums[0:16] / col_sum[None, :]

    with jax.named_scope("row_sums"):
        rows = row_sums(src_points, tgt_points, tgt_term[None, :])
    with jax.named_scope("map_combine"):
        parts = rows.reshape(24, -1, share).transpose(1, 0, 2)
        parts = lax.all_to_all(parts, "tgt", 0, 0)
        peaks = parts[:, 0]
        factor = jnp.exp2(peaks - jnp.max(peaks, 0))
        row_sum = jnp.sum(parts[:, 1] * factor, 0)
        src_map = jnp.sum(parts[:, 8:24] * factor[:, None, :], 0) / row_sum[None, :]
    return (f_new, g_new, src_map, tgt_map)


def solution(mesh):
    in_specs = (P(None, "src"), P(None, "tgt"), P("src"), P("tgt"), P("tgt"))
    out_specs = (P("src"), P("tgt"), P(None, ("src", "tgt")), P(None, "tgt"))
    return jax.shard_map(
        per_device, mesh=mesh, in_specs=in_specs, out_specs=out_specs, check_vma=False
    )
```

```python
import functools
import math

import jax
import jax.numpy as jnp
from jax import lax
from jax.experimental import pallas as pl
from jax.experimental.pallas import tpu as pltpu
from jax.sharding import PartitionSpec as P

LOG2E = math.log2(math.e)
LN2 = math.log(2.0)
ENTROPY = 4.0
ALPHA = LOG2E / ENTROPY
ROWS = 1024
LANES = 256
WIDE = 1024
HEAD = 128
DEPTH = 128
LOWEST = -1e30
bf16 = jnp.bfloat16
f32 = jnp.float32

Y_MASKS = (1, 3)
Z_MASKS = (4, 8, 24)
SRC_MASKS = (1, 2, 6)


def split3(values):
    first = values.astype(bf16).astype(f32)
    rest = values - first
    second = rest.astype(bf16).astype(f32)
    third = (rest - second).astype(bf16).astype(f32)
    return first, second, third


def stack_terms(points, potential):
    n = points.shape[1]
    a, b, c = split3(points)
    u, v, w = split3(potential)
    row = lax.broadcasted_iota(jnp.int32, (16, n), 0)
    extra = jnp.where(row == 0, u, jnp.where(row == 1, v, jnp.where(row == 2, w, 0.0)))
    return jnp.concatenate([a, b, c, a, b, a, extra, jnp.zeros((16, n), f32)], 0)


def stack_plain(points):
    n = points.shape[1]
    a, b, c = (part.astype(bf16) for part in split3(points))
    ones = jnp.ones((16, n), bf16)
    return jnp.concatenate([a, a, a, b, b, c, ones, jnp.zeros((16, n), bf16)], 0)


def column_max(x_ref, rows):
    peak = x_ref[0:16, :]
    for at in range(16, rows, 16):
        peak = jnp.maximum(peak, x_ref[at : at + 16, :])
    return jnp.max(peak, axis=0, keepdims=True)


def lse_kernel(
    src_ref, tgt_ref, g_ref, out_ref, rows_ref, cols_ref, x0_ref, x1_ref, sum_ref
):
    tgt = tgt_ref[...]
    term = ALPHA * (g_ref[...] - jnp.sum(tgt * tgt, axis=0, keepdims=True))
    rows_ref[...] = stack_terms(tgt, term).T.astype(bf16)
    cols_ref[...] = stack_plain(src_ref[...] * (2.0 * ALPHA))
    tiles = src_ref.shape[1] // WIDE
    slots = (x0_ref, x1_ref)

    def product(tile, x_ref):
        at = pl.multiple_of(tile * WIDE, WIDE)
        x_ref[...] = jnp.dot(
            rows_ref[...], cols_ref[:, pl.ds(at, WIDE)], preferred_element_type=f32
        )

    def reduce(tile, x_ref, depth):
        at = pl.multiple_of(tile * WIDE, WIDE)
        shift = column_max(x_ref, depth)
        total = jnp.zeros((16, WIDE), f32)
        for i in range(0, ROWS, 16):
            total = total + jnp.exp2(x_ref[i : i + 16, :] - shift)
        total = jnp.sum(total, axis=0, keepdims=True)
        out_ref[:, pl.ds(at, WIDE)] = shift + jnp.log2(total)
        sum_ref[:, pl.ds(at, WIDE)] = total

    product(0, x0_ref)

    def body(pair, carry):
        for slot in range(2):
            tile = pair * 2 + slot
            product(jnp.minimum(tile + 1, tiles - 1), slots[1 - slot])
            reduce(tile, slots[slot], HEAD)
        return carry

    lax.fori_loop(0, tiles // 2, body, 0)

    def again(tile, carry):
        at = pl.multiple_of(tile * WIDE, WIDE)

        @pl.when(jnp.logical_not(jnp.max(sum_ref[:, pl.ds(at, WIDE)]) < 2.0**100))
        def _():
            product(tile, x0_ref)
            reduce(tile, x0_ref, ROWS)

        return carry

    lax.fori_loop(0, tiles, again, 0)


def two_parts(points):
    first = points.astype(bf16)
    second = (points - first.astype(f32)).astype(bf16)
    return jnp.concatenate([first, jnp.ones(points.shape, bf16), second], 0)


def sums_kernel(
    rows_in_ref, cols_in_ref, term_ref, out_ref, r0_ref, r1_ref, b0_ref, b1_ref, cols_ref, x0_ref, x1_ref, hi_ref, lo_ref
):
    blocks = rows_in_ref.shape[1] // ROWS
    width = cols_in_ref.shape[1]
    tiles = width // LANES
    sides = (r0_ref, r1_ref)
    boths = (b0_ref, b1_ref)
    slots = (x0_ref, x1_ref)
    cols_ref[...] = stack_plain(cols_in_ref[...] * (2.0 * ALPHA))

    def build(block, side, first, last):
        at = pl.multiple_of(block * ROWS + first, LANES)
        points = rows_in_ref[:, pl.ds(at, last - first)]
        term = term_ref[:, pl.ds(at, last - first)]
        sides[side][first:last, :] = stack_terms(points, term).T.astype(bf16)
        boths[side][:, first:last] = two_parts(points)

    def product(side, tile, x_ref):
        x_ref[...] = jnp.dot(
            sides[side][...],
            cols_ref[:, tile * LANES : (tile + 1) * LANES],
            preferred_element_type=f32,
        )

    def accumulate(side, tile, x_ref):
        peak = column_max(x_ref, ROWS)
        for at in range(0, ROWS, 128):
            weights = jnp.exp2(x_ref[at : at + 128, :] - peak)
            hi = weights.astype(bf16)
            hi_ref[at : at + 128, :] = hi
            lo_ref[at : at + 128, :] = (weights - hi.astype(f32)).astype(bf16)
        both = boths[side][...]
        big = jnp.dot(both, hi_ref[...], preferred_element_type=f32)
        small = jnp.dot(both[0:32], lo_ref[...], preferred_element_type=f32)
        here = slice(tile * LANES, (tile + 1) * LANES)
        before = out_ref[0:1, here]
        after = jnp.maximum(before, peak)
        old = jnp.exp2(before - after)
        new = jnp.exp2(peak - after)
        total = out_ref[0:8, here] * old + (big[16:24] + small[16:24]) * new
        row = lax.broadcasted_iota(jnp.int32, (8, LANES), 0)
        out_ref[0:8, here] = jnp.where(row == 0, after, total)
        mass = big[0:16] + big[32:48] + small[0:16]
        out_ref[8:24, here] = out_ref[8:24, here] * old + mass * new

    row = lax.broadcasted_iota(jnp.int32, (24, width), 0)
    out_ref[...] = jnp.where(row == 0, LOWEST, 0.0)
    build(0, 0, 0, ROWS)
    product(0, 0, x0_ref)

    def body(pair, carry):
        for side in range(2):
            block = pair * 2 + side
            after = jnp.minimum(block + 1, blocks - 1)
            for tile in range(tiles):
                if tile < 2:
                    build(after, 1 - side, tile * ROWS // 2, (tile + 1) * ROWS // 2)
                later = slots[(tile + 1) % 2]
                if tile + 1 < tiles:
                    product(side, tile + 1, later)
                else:
                    product(1 - side, 0, later)
                accumulate(side, tile, slots[tile % 2])
        return carry

    lax.fori_loop(0, blocks // 2, body, 0)


params = pltpu.CompilerParams(vmem_limit_bytes=48 * 1024 * 1024)
vmem = pl.BlockSpec(memory_space=pltpu.VMEM)


def cost(rows, columns):
    pairs = rows * columns
    return pl.CostEstimate(
        flops=600 * pairs, transcendentals=pairs, bytes_accessed=64 * (rows + columns)
    )


def row_lse(src, tgt, g):
    n, k = src.shape[1], tgt.shape[1]
    return pl.pallas_call(
        lse_kernel,
        out_shape=jax.ShapeDtypeStruct((1, n), f32),
        in_specs=[vmem] * 3,
        out_specs=vmem,
        scratch_shapes=[
            pltpu.VMEM((k, DEPTH), bf16),
            pltpu.VMEM((DEPTH, n), bf16),
            pltpu.VMEM((ROWS, WIDE), f32),
            pltpu.VMEM((ROWS, WIDE), f32),
            pltpu.VMEM((1, n), f32),
        ],
        compiler_params=params,
        cost_estimate=cost(n, k),
        name="row_lse",
    )(src, tgt, g)


def weighted_sums(rows, columns, term):
    n, k = rows.shape[1], columns.shape[1]
    return pl.pallas_call(
        sums_kernel,
        out_shape=jax.ShapeDtypeStruct((24, k), f32),
        in_specs=[vmem] * 3,
        out_specs=vmem,
        scratch_shapes=[
            pltpu.VMEM((ROWS, DEPTH), bf16),
            pltpu.VMEM((ROWS, DEPTH), bf16),
            pltpu.VMEM((48, ROWS), bf16),
            pltpu.VMEM((48, ROWS), bf16),
            pltpu.VMEM((DEPTH, k), bf16),
            pltpu.VMEM((ROWS, LANES), f32),
            pltpu.VMEM((ROWS, LANES), f32),
            pltpu.VMEM((ROWS, LANES), bf16),
            pltpu.VMEM((ROWS, LANES), bf16),
        ],
        compiler_params=params,
        cost_estimate=cost(n, k),
        name="weighted_sums",
    )(rows, columns, term)


def swap(values, axis, mask):
    size = lax.axis_size(axis)
    return lax.ppermute(values, axis, [(i, i ^ mask) for i in range(size)])


def merge(mine, theirs):
    top = jnp.maximum(mine[0:1], theirs[0:1])
    sums = mine * jnp.exp2(mine[0:1] - top) + theirs * jnp.exp2(theirs[0:1] - top)
    row = lax.broadcasted_iota(jnp.int32, mine.shape, 0)
    return jnp.where(row == 0, top, sums)


def per_device(src_points, tgt_points, log_a, log_b, g_init):
    place = lax.axis_index("tgt")
    share = src_points.shape[1] // lax.axis_size("tgt")
    picks = [
        lax.dynamic_slice_in_dim(src_points, (place ^ k) * share, share, 1)
        for k in (0, 1, 3, 2)
    ]
    part = jnp.concatenate(picks, 1)

    with jax.named_scope("gather_points_1"):
        near = jnp.concatenate([tgt_points, swap(tgt_points, "tgt", Z_MASKS[0])], 1)
    with jax.named_scope("row_lse"):
        level = row_lse(src_points, tgt_points, g_init[None, :])[0]
    with jax.named_scope("gather_points_2"):
        near, level = lax.optimization_barrier((near, level))
        near = jnp.concatenate([near, swap(near, "tgt", Z_MASKS[1])], 1)
    with jax.named_scope("row_combine"):
        for mask in Y_MASKS + Z_MASKS:
            other = swap(level, "tgt", mask)
            level = jnp.maximum(level, other) + jnp.log2(
                1.0 + jnp.exp2(-jnp.abs(level - other))
            )
        src_term = LOG2E * log_a - level
        f_new = ENTROPY * LN2 * src_term + jnp.sum(src_points * src_points, 0)

    with jax.named_scope("gather_points_3"):
        near, src_term = lax.optimization_barrier((near, src_term))
        far = swap(near, "tgt", Z_MASKS[2])
    with jax.named_scope("column_sums"):
        columns = weighted_sums(src_points, tgt_points, src_term[None, :])
        columns, far = lax.optimization_barrier((columns, far))
    with jax.named_scope("column_combine"):
        for mask in SRC_MASKS:
            columns = merge(columns, swap(columns, "src", mask))
        tgt_term = LOG2E * log_b - columns[0] - jnp.log2(columns[1])
        g_new = ENTROPY * LN2 * tgt_term + jnp.sum(tgt_points * tgt_points, 0)
        tgt_map = columns[8:24] / columns[1:2]

    with jax.named_scope("gather_term"):
        term = tgt_term[None, :]
        for mask in Z_MASKS[:2]:
            term = jnp.concatenate([term, swap(term, "tgt", mask)], 1)
        far_term = swap(term, "tgt", Z_MASKS[2])
    with jax.named_scope("row_sums"):
        rows = weighted_sums(near, part, term)
        rows = merge(rows, weighted_sums(far, part, far_term))
    with jax.named_scope("map_combine"):
        half = 2 * share
        rows = merge(rows[:, :half], swap(rows[:, half:], "tgt", Y_MASKS[1]))
        rows = merge(rows[:, :share], swap(rows[:, share:], "tgt", Y_MASKS[0]))
        src_map = rows[8:24] / rows[1:2]
    return (f_new, g_new, src_map, tgt_map)


def solution(mesh):
    in_specs = (P(None, "src"), P(None, "tgt"), P("src"), P("tgt"), P("tgt"))
    out_specs = (P("src"), P("tgt"), P(None, ("src", "tgt")), P(None, "tgt"))
    return jax.shard_map(
        per_device, mesh=mesh, in_specs=in_specs, out_specs=out_specs, check_vma=False
    )
```

```python
import functools
import math

import jax
import jax.numpy as jnp
from jax import lax
from jax.experimental import pallas as pl
from jax.experimental.pallas import tpu as pltpu
from jax.sharding import PartitionSpec as P

LOG2E = math.log2(math.e)
LN2 = math.log(2.0)
ENTROPY = 4.0
ALPHA = LOG2E / ENTROPY
ROWS = 1024
LANES = 256
WIDE = 1024
HEAD = 128
DEPTH = 128
LOWEST = -1e30
bf16 = jnp.bfloat16
f32 = jnp.float32

Y_MASKS = (1, 3)
Z_MASKS = (4, 8, 24)
SRC_MASKS = (1, 3, 7)


def split3(values):
    first = values.astype(bf16).astype(f32)
    rest = values - first
    second = rest.astype(bf16).astype(f32)
    third = (rest - second).astype(bf16).astype(f32)
    return first, second, third


def stack_terms(points, potential):
    n = points.shape[1]
    a, b, c = split3(points)
    u, v, w = split3(potential)
    row = lax.broadcasted_iota(jnp.int32, (16, n), 0)
    extra = jnp.where(row == 0, u, jnp.where(row == 1, v, jnp.where(row == 2, w, 0.0)))
    return jnp.concatenate([a, b, c, a, b, a, extra, jnp.zeros((16, n), f32)], 0)


def stack_plain(points):
    n = points.shape[1]
    a, b, c = (part.astype(bf16) for part in split3(points))
    ones = jnp.ones((16, n), bf16)
    return jnp.concatenate([a, a, a, b, b, c, ones, jnp.zeros((16, n), bf16)], 0)


def column_max(x_ref, rows):
    peak = x_ref[0:16, :]
    for at in range(16, rows, 16):
        peak = jnp.maximum(peak, x_ref[at : at + 16, :])
    return jnp.max(peak, axis=0, keepdims=True)


def lse_kernel(
    src_ref, tgt_ref, g_ref, out_ref, rows_ref, cols_ref, x0_ref, x1_ref, sum_ref
):
    tgt = tgt_ref[...]
    term = ALPHA * (g_ref[...] - jnp.sum(tgt * tgt, axis=0, keepdims=True))
    rows_ref[...] = stack_terms(tgt, term).T.astype(bf16)
    cols_ref[...] = stack_plain(src_ref[...] * (2.0 * ALPHA))
    tiles = src_ref.shape[1] // WIDE
    slots = (x0_ref, x1_ref)

    def product(tile, x_ref):
        at = pl.multiple_of(tile * WIDE, WIDE)
        x_ref[...] = jnp.dot(
            rows_ref[...], cols_ref[:, pl.ds(at, WIDE)], preferred_element_type=f32
        )

    def reduce(tile, x_ref, depth):
        at = pl.multiple_of(tile * WIDE, WIDE)
        shift = column_max(x_ref, depth)
        total = jnp.zeros((16, WIDE), f32)
        for i in range(0, ROWS, 16):
            total = total + jnp.exp2(x_ref[i : i + 16, :] - shift)
        total = jnp.sum(total, axis=0, keepdims=True)
        out_ref[:, pl.ds(at, WIDE)] = shift + jnp.log2(total)
        sum_ref[:, pl.ds(at, WIDE)] = total

    product(0, x0_ref)

    def body(pair, carry):
        for slot in range(2):
            tile = pair * 2 + slot
            product(jnp.minimum(tile + 1, tiles - 1), slots[1 - slot])
            reduce(tile, slots[slot], HEAD)
        return carry

    lax.fori_loop(0, tiles // 2, body, 0)

    def again(tile, carry):
        at = pl.multiple_of(tile * WIDE, WIDE)

        @pl.when(jnp.logical_not(jnp.max(sum_ref[:, pl.ds(at, WIDE)]) < 2.0**100))
        def _():
            product(tile, x0_ref)
            reduce(tile, x0_ref, ROWS)

        return carry

    lax.fori_loop(0, tiles, again, 0)


def two_parts(points):
    first = points.astype(bf16)
    second = (points - first.astype(f32)).astype(bf16)
    return jnp.concatenate([first, jnp.ones(points.shape, bf16), second], 0)


def sums_kernel(
    rows_in_ref, cols_in_ref, term_ref, out_ref, r0_ref, r1_ref, b0_ref, b1_ref, cols_ref, x0_ref, x1_ref, high_ref
):
    blocks = rows_in_ref.shape[1] // ROWS
    width = cols_in_ref.shape[1]
    tiles = width // LANES
    parts = min(tiles, 2)
    sides = (r0_ref, r1_ref)
    boths = (b0_ref, b1_ref)
    slots = (x0_ref, x1_ref)
    cols_ref[...] = stack_plain(cols_in_ref[...] * (2.0 * ALPHA))

    def build(block, side, first, last):
        at = pl.multiple_of(block * ROWS + first, LANES)
        points = rows_in_ref[:, pl.ds(at, last - first)]
        term = term_ref[:, pl.ds(at, last - first)]
        sides[side][first:last, :] = stack_terms(points, term).T.astype(bf16)
        boths[side][:, first:last] = two_parts(points)

    def product(side, tile, x_ref):
        x_ref[...] = jnp.dot(
            sides[side][...],
            cols_ref[:, tile * LANES : (tile + 1) * LANES],
            preferred_element_type=f32,
        )

    def accumulate(side, tile, x_ref, depth):
        shift = column_max(x_ref, depth)
        big = jnp.zeros((48, LANES), f32)
        small = jnp.zeros((32, LANES), f32)
        for at in range(0, ROWS, 256):
            weights = jnp.exp2(x_ref[at : at + 256, :] - shift)
            hi = weights.astype(bf16)
            lo = (weights - hi.astype(f32)).astype(bf16)
            both = boths[side][:, at : at + 256]
            big += jnp.dot(both, hi, preferred_element_type=f32)
            small += jnp.dot(both[0:32], lo, preferred_element_type=f32)
        high_ref[...] = jnp.maximum(high_ref[...], big[16:24])
        here = slice(tile * LANES, (tile + 1) * LANES)
        before = out_ref[0:1, here]
        after = jnp.maximum(before, shift)
        old = jnp.exp2(before - after)
        new = jnp.exp2(shift - after)
        total = out_ref[0:8, here] * old + (big[16:24] + small[16:24]) * new
        row = lax.broadcasted_iota(jnp.int32, (8, LANES), 0)
        out_ref[0:8, here] = jnp.where(row == 0, after, total)
        mass = big[0:16] + big[32:48] + small[0:16]
        out_ref[8:24, here] = out_ref[8:24, here] * old + mass * new

    def run(depth):
        row = lax.broadcasted_iota(jnp.int32, (24, width), 0)
        out_ref[...] = jnp.where(row == 0, LOWEST, 0.0)
        high_ref[...] = jnp.zeros((8, LANES), f32)
        build(0, 0, 0, ROWS)
        product(0, 0, x0_ref)

        def body(pair, carry):
            for step in range(2 * tiles):
                side, tile = divmod(step, tiles)
                after = jnp.minimum(pair * 2 + side + 1, blocks - 1)
                if tile < parts:
                    build(after, 1 - side, tile * ROWS // parts, (tile + 1) * ROWS // parts)
                later = slots[(step + 1) % 2]
                if tile + 1 < tiles:
                    product(side, tile + 1, later)
                else:
                    product(1 - side, 0, later)
                accumulate(side, tile, slots[step % 2], depth)
            return carry

        lax.fori_loop(0, blocks // 2, body, 0)

    run(HEAD)

    @pl.when(jnp.logical_not(jnp.max(high_ref[...]) < 2.0**60))
    def _():
        run(ROWS)


params = pltpu.CompilerParams(vmem_limit_bytes=48 * 1024 * 1024)
vmem = pl.BlockSpec(memory_space=pltpu.VMEM)


def cost(rows, columns):
    pairs = rows * columns
    return pl.CostEstimate(
        flops=1500 * pairs, transcendentals=pairs, bytes_accessed=64 * (rows + columns)
    )


def row_lse(src, tgt, g):
    n, k = src.shape[1], tgt.shape[1]
    return pl.pallas_call(
        lse_kernel,
        out_shape=jax.ShapeDtypeStruct((1, n), f32),
        in_specs=[vmem] * 3,
        out_specs=vmem,
        scratch_shapes=[
            pltpu.VMEM((k, DEPTH), bf16),
            pltpu.VMEM((DEPTH, n), bf16),
            pltpu.VMEM((ROWS, WIDE), f32),
            pltpu.VMEM((ROWS, WIDE), f32),
            pltpu.VMEM((1, n), f32),
        ],
        compiler_params=params,
        cost_estimate=cost(n, k),
        name="row_lse",
    )(src, tgt, g)


def weighted_sums(rows, columns, term):
    n, k = rows.shape[1], columns.shape[1]
    return pl.pallas_call(
        sums_kernel,
        out_shape=jax.ShapeDtypeStruct((24, k), f32),
        in_specs=[vmem] * 3,
        out_specs=vmem,
        scratch_shapes=[
            pltpu.VMEM((ROWS, DEPTH), bf16),
            pltpu.VMEM((ROWS, DEPTH), bf16),
            pltpu.VMEM((48, ROWS), bf16),
            pltpu.VMEM((48, ROWS), bf16),
            pltpu.VMEM((DEPTH, k), bf16),
            pltpu.VMEM((ROWS, LANES), f32),
            pltpu.VMEM((ROWS, LANES), f32),
            pltpu.VMEM((8, LANES), f32),
        ],
        compiler_params=params,
        cost_estimate=cost(n, k),
        name="weighted_sums",
    )(rows, columns, term)


def swap(values, src_mask, tgt_mask):
    width = lax.axis_size("tgt")
    size = width * lax.axis_size("src")
    mask = src_mask * width + tgt_mask
    return lax.ppermute(values, ("src", "tgt"), [(i, i ^ mask) for i in range(size)])


def merge(mine, theirs):
    top = jnp.maximum(mine[0:1], theirs[0:1])
    sums = mine * jnp.exp2(mine[0:1] - top) + theirs * jnp.exp2(theirs[0:1] - top)
    row = lax.broadcasted_iota(jnp.int32, mine.shape, 0)
    return jnp.where(row == 0, top, sums)


def per_device(src_points, tgt_points, log_a, log_b, g_init):
    place = lax.axis_index("tgt")
    share = src_points.shape[1] // lax.axis_size("tgt")
    picks = [
        lax.dynamic_slice_in_dim(src_points, (place ^ k) * share, share, 1)
        for k in range(4)
    ]
    part = jnp.concatenate(picks, 1)

    crossed = (place ^ (place >> 2) ^ (place >> 3)) & 1 == 1
    with jax.named_scope("cross"):
        sources = jnp.where(crossed, swap(src_points, 1, 0), src_points)
        masses = LOG2E * jnp.where(crossed, swap(log_a, 1, 0), log_a)
    with jax.named_scope("gather_points_1"):
        more = swap(tgt_points, 1, Z_MASKS[0])
    with jax.named_scope("row_lse"):
        level = row_lse(sources, tgt_points, g_init[None, :])[0]
        more, level, masses = lax.optimization_barrier((more, level, masses))
        near = jnp.concatenate([tgt_points, more], 1)
    with jax.named_scope("row_combine"):
        for mask in Y_MASKS + Z_MASKS:
            other = swap(level, 1, mask)
            level = jnp.maximum(level, other) + jnp.log2(
                1.0 + jnp.exp2(-jnp.abs(level - other))
            )
        src_term = masses - level
    with jax.named_scope("gather_points_2"):
        near, src_term = lax.optimization_barrier((near, src_term))
        more = swap(near, 1, Z_MASKS[1])
    with jax.named_scope("column_sums"):
        columns = weighted_sums(sources, tgt_points, src_term[None, :])
        columns, more, level = lax.optimization_barrier((columns, more, level))
    with jax.named_scope("gather_points_3"):
        near = jnp.concatenate([near, more], 1)
        far = swap(near, 1, Z_MASKS[2])
    with jax.named_scope("row_results"):
        level = jnp.where(crossed, swap(level, 1, 0), level)
        f_new = ENTROPY * LN2 * (LOG2E * log_a - level) + jnp.sum(src_points * src_points, 0)
    with jax.named_scope("column_combine"):
        tgt_mass = LOG2E * log_b
        for step, mask in enumerate(SRC_MASKS):
            if step == 2:
                columns, tgt_mass = lax.optimization_barrier((columns, tgt_mass))
            columns = merge(columns, swap(columns, mask, 0))
        tgt_term = tgt_mass - columns[0] - jnp.log2(columns[1])

    with jax.named_scope("gather_term"):
        term = tgt_term[None, :]
        term = jnp.concatenate([term, swap(term, 1, Z_MASKS[0])], 1)
        term, columns, tgt_term = lax.optimization_barrier((term, columns, tgt_term))
        term = jnp.concatenate([term, swap(term, 1, Z_MASKS[1])], 1)
        far_term = swap(term, 1, Z_MASKS[2])
    with jax.named_scope("column_results"):
        g_new = ENTROPY * LN2 * tgt_term + jnp.sum(tgt_points * tgt_points, 0)
        tgt_map = columns[8:24] / columns[1:2]
    with jax.named_scope("row_sums"):
        rows = weighted_sums(near, part, term)
        rows, far = lax.optimization_barrier((rows, far))
    with jax.named_scope("map_combine"):
        away = merge(rows[:, share:], weighted_sums(far, part[:, share:], far_term))
        away, far_term = lax.optimization_barrier((away, far_term))
        arrived = [
            swap(away[:, k * share : (k + 1) * share], 0, k + 1) for k in range(3)
        ]
        others = merge(merge(arrived[0], arrived[2]), arrived[1])
        mine = weighted_sums(far, part[:, :share], far_term)
        rows = merge(merge(rows[:, :share], others), mine)
        src_map = rows[8:24] / rows[1:2]
    return (f_new, g_new, src_map, tgt_map)


def solution(mesh):
    in_specs = (P(None, "src"), P(None, "tgt"), P("src"), P("tgt"), P("tgt"))
    out_specs = (P("src"), P("tgt"), P(None, ("src", "tgt")), P(None, "tgt"))
    return jax.shard_map(
        per_device, mesh=mesh, in_specs=in_specs, out_specs=out_specs, check_vma=False
    )
```

```python
import functools
import math

import jax
import jax.numpy as jnp
from jax import lax
from jax.experimental import pallas as pl
from jax.experimental.pallas import tpu as pltpu
from jax.sharding import PartitionSpec as P

LOG2E = math.log2(math.e)
LN2 = math.log(2.0)
ENTROPY = 4.0
ALPHA = LOG2E / ENTROPY
ROWS = 1024
LANES = 256
WIDE = 1024
HEAD = 128
DEPTH = 128
LOWEST = -1e30
bf16 = jnp.bfloat16
f32 = jnp.float32

T_MASKS = (4, 8, 24)
Z_MASKS = (8, 24, 4)
SRC_MASKS = (1, 3, 7)


def split3(values):
    first = values.astype(bf16).astype(f32)
    rest = values - first
    second = rest.astype(bf16).astype(f32)
    third = (rest - second).astype(bf16).astype(f32)
    return first, second, third


def stack_terms(points, potential):
    n = points.shape[1]
    a, b, c = split3(points)
    u, v, w = split3(potential)
    row = lax.broadcasted_iota(jnp.int32, (16, n), 0)
    extra = jnp.where(row == 0, u, jnp.where(row == 1, v, jnp.where(row == 2, w, 0.0)))
    return jnp.concatenate([a, b, c, a, b, a, extra, jnp.zeros((16, n), f32)], 0)


def stack_plain(points):
    n = points.shape[1]
    a, b, c = (part.astype(bf16) for part in split3(points))
    ones = jnp.ones((16, n), bf16)
    return jnp.concatenate([a, a, a, b, b, c, ones, jnp.zeros((16, n), bf16)], 0)


def column_max(x_ref, rows):
    peak = x_ref[0:16, :]
    for at in range(16, rows, 16):
        peak = jnp.maximum(peak, x_ref[at : at + 16, :])
    return jnp.max(peak, axis=0, keepdims=True)


def lse_kernel(
    flag_ref, own_ref, other_ref, tgt_ref, g_ref, out_ref, rows_ref, cols_ref, x0_ref, x1_ref, sum_ref
):
    tgt = tgt_ref[...]
    term = ALPHA * (g_ref[...] - jnp.sum(tgt * tgt, axis=0, keepdims=True))
    rows_ref[...] = stack_terms(tgt, term).T.astype(bf16)
    src = jnp.where(flag_ref[0] != 0, other_ref[...], own_ref[...])
    cols_ref[...] = stack_plain(src * (2.0 * ALPHA))
    tiles = own_ref.shape[1] // WIDE
    slots = (x0_ref, x1_ref)

    def product(tile, x_ref):
        at = pl.multiple_of(tile * WIDE, WIDE)
        x_ref[...] = jnp.dot(
            rows_ref[...], cols_ref[:, pl.ds(at, WIDE)], preferred_element_type=f32
        )

    def reduce(tile, x_ref, depth):
        at = pl.multiple_of(tile * WIDE, WIDE)
        shift = column_max(x_ref, depth)
        total = jnp.zeros((16, WIDE), f32)
        for i in range(0, ROWS, 16):
            total = total + jnp.exp2(x_ref[i : i + 16, :] - shift)
        total = jnp.sum(total, axis=0, keepdims=True)
        out_ref[:, pl.ds(at, WIDE)] = shift + jnp.log2(total)
        sum_ref[:, pl.ds(at, WIDE)] = total

    product(0, x0_ref)

    def body(pair, carry):
        for slot in range(2):
            tile = pair * 2 + slot
            product(jnp.minimum(tile + 1, tiles - 1), slots[1 - slot])
            reduce(tile, slots[slot], HEAD)
        return carry

    lax.fori_loop(0, tiles // 2, body, 0)

    def again(tile, carry):
        at = pl.multiple_of(tile * WIDE, WIDE)

        @pl.when(jnp.logical_not(jnp.max(sum_ref[:, pl.ds(at, WIDE)]) < 2.0**100))
        def _():
            product(tile, x0_ref)
            reduce(tile, x0_ref, ROWS)

        return carry

    lax.fori_loop(0, tiles, again, 0)


def two_parts(points):
    first = points.astype(bf16)
    second = (points - first.astype(f32)).astype(bf16)
    return jnp.concatenate([first, jnp.ones(points.shape, bf16), second], 0)


def sums_kernel(arrays, picked, flag_ref, *refs):
    rows_in = refs[: arrays + picked]
    terms = refs[arrays + picked : 2 * arrays + picked]
    cols_in_ref, out_ref, r0_ref, r1_ref, b0_ref, b1_ref, cols_ref, x0_ref, x1_ref, high_ref = refs[
        2 * arrays + picked :
    ]
    each = rows_in[0].shape[1] // ROWS
    blocks = each * arrays
    width = cols_in_ref.shape[1]
    tiles = width // LANES
    unrolled = blocks * tiles <= 8
    sides = (r0_ref, r1_ref)
    boths = (b0_ref, b1_ref)
    slots = (x0_ref, x1_ref)
    cols_ref[...] = stack_plain(cols_in_ref[...] * (2.0 * ALPHA))

    def load(block, first, last):
        array = block // each if arrays > 1 else 0
        at = (block - array * each) * ROWS + first
        if not isinstance(at, int):
            at = pl.multiple_of(at, LANES)
        where = pl.ds(at, last - first)
        points = rows_in[array][:, where]
        if picked:
            points = jnp.where(flag_ref[0] != 0, rows_in[1][:, where], points)
        return points, terms[array][:, where]

    def build_side(block, side, first, last):
        points, term = load(block, first, last)
        sides[side][first:last, :] = stack_terms(points, term).T.astype(bf16)

    def build_both(block, side, first, last):
        boths[side][:, first:last] = two_parts(load(block, first, last)[0])

    def product(side, tile, x_ref):
        x_ref[...] = jnp.dot(
            sides[side][...],
            cols_ref[:, tile * LANES : (tile + 1) * LANES],
            preferred_element_type=f32,
        )

    def accumulate(side, tile, x_ref, depth):
        shift = column_max(x_ref, depth)
        big = jnp.zeros((48, LANES), f32)
        small = jnp.zeros((32, LANES), f32)
        for at in range(0, ROWS, 256):
            weights = jnp.exp2(x_ref[at : at + 256, :] - shift)
            hi = weights.astype(bf16)
            lo = (weights - hi.astype(f32)).astype(bf16)
            both = boths[side][:, at : at + 256]
            big += jnp.dot(both, hi, preferred_element_type=f32)
            small += jnp.dot(both[0:32], lo, preferred_element_type=f32)
        high_ref[...] = jnp.maximum(high_ref[...], big[16:24])
        here = slice(tile * LANES, (tile + 1) * LANES)
        before = out_ref[0:1, here]
        after = jnp.maximum(before, shift)
        old = jnp.exp2(before - after)
        new = jnp.exp2(shift - after)
        total = out_ref[0:8, here] * old + (big[16:24] + small[16:24]) * new
        row = lax.broadcasted_iota(jnp.int32, (8, LANES), 0)
        out_ref[0:8, here] = jnp.where(row == 0, after, total)
        mass = big[0:16] + big[32:48] + small[0:16]
        out_ref[8:24, here] = out_ref[8:24, here] * old + mass * new

    def run(depth):
        row = lax.broadcasted_iota(jnp.int32, (24, width), 0)
        out_ref[...] = jnp.where(row == 0, LOWEST, 0.0)
        high_ref[...] = jnp.zeros((8, LANES), f32)
        build_side(0, 0, 0, ROWS)
        build_both(0, 0, 0, ROWS)
        product(0, 0, x0_ref)
        if tiles == 1:
            build_side(1, 1, 0, ROWS)

        def body(pair, carry):
            for step in range(2 * tiles):
                side, tile = divmod(step, tiles)
                block = pair * 2 + side
                later = slots[(step + 1) % 2]
                if isinstance(block, int):
                    after, second = min(block + 1, blocks - 1), min(block + 2, blocks - 1)
                    final = block == blocks - 1
                else:
                    after, final = jnp.minimum(block + 1, blocks - 1), False
                if not final:
                    if tiles == 1:
                        build_both(after, 1 - side, 0, ROWS)
                    elif tile < 2 and tiles > 2:
                        first, last = tile * ROWS // 2, (tile + 1) * ROWS // 2
                        build_side(after, 1 - side, first, last)
                        build_both(after, 1 - side, first, last)
                    elif tile == 0:
                        build_side(after, 1 - side, 0, ROWS)
                        build_both(after, 1 - side, 0, ROWS)
                if tile + 1 < tiles:
                    product(side, tile + 1, later)
                elif not final:
                    product(1 - side, 0, later)
                    if tiles == 1 and block + 2 < blocks:
                        build_side(second, side, 0, ROWS)
                accumulate(side, tile, slots[step % 2], depth)
            return carry

        if unrolled:
            for pair in range(blocks // 2):
                body(pair, 0)
        else:
            lax.fori_loop(0, blocks // 2, body, 0)

    run(HEAD)

    @pl.when(jnp.logical_not(jnp.max(high_ref[...]) < 2.0**60))
    def _():
        run(ROWS)


params = pltpu.CompilerParams(vmem_limit_bytes=48 * 1024 * 1024)
vmem = pl.BlockSpec(memory_space=pltpu.VMEM)
scalars = pl.BlockSpec(memory_space=pltpu.SMEM)


def cost(rows, columns):
    pairs = rows * columns
    return pl.CostEstimate(
        flops=1500 * pairs, transcendentals=pairs, bytes_accessed=64 * (rows + columns)
    )


def row_lse(flag, own, other, tgt, g):
    n, k = own.shape[1], tgt.shape[1]
    return pl.pallas_call(
        lse_kernel,
        out_shape=jax.ShapeDtypeStruct((1, n), f32),
        in_specs=[scalars] + [vmem] * 4,
        out_specs=vmem,
        scratch_shapes=[
            pltpu.VMEM((k, DEPTH), bf16),
            pltpu.VMEM((DEPTH, n), bf16),
            pltpu.VMEM((ROWS, WIDE), f32),
            pltpu.VMEM((ROWS, WIDE), f32),
            pltpu.VMEM((1, n), f32),
        ],
        compiler_params=params,
        cost_estimate=cost(n, k),
        name="row_lse",
    )(flag, own, other, tgt, g)


def weighted_sums(flag, rows, terms, columns):
    n, k = rows[0].shape[1], columns.shape[1]
    arrays, picked = len(terms), len(rows) - len(terms)
    return pl.pallas_call(
        functools.partial(sums_kernel, arrays, picked),
        out_shape=jax.ShapeDtypeStruct((24, k), f32),
        in_specs=[scalars] + [vmem] * (len(rows) + len(terms) + 1),
        out_specs=vmem,
        scratch_shapes=[
            pltpu.VMEM((ROWS, DEPTH), bf16),
            pltpu.VMEM((ROWS, DEPTH), bf16),
            pltpu.VMEM((48, ROWS), bf16),
            pltpu.VMEM((48, ROWS), bf16),
            pltpu.VMEM((DEPTH, k), bf16),
            pltpu.VMEM((ROWS, LANES), f32),
            pltpu.VMEM((ROWS, LANES), f32),
            pltpu.VMEM((8, LANES), f32),
        ],
        compiler_params=params,
        cost_estimate=cost(n * arrays, k),
        name="weighted_sums",
    )(flag, *rows, *terms, columns)


def swap(values, src_mask, tgt_mask):
    width = lax.axis_size("tgt")
    size = width * lax.axis_size("src")
    mask = src_mask * width + tgt_mask
    return lax.ppermute(values, ("src", "tgt"), [(i, i ^ mask) for i in range(size)])


def merge(mine, theirs):
    top = jnp.maximum(mine[0:1], theirs[0:1])
    sums = mine * jnp.exp2(mine[0:1] - top) + theirs * jnp.exp2(theirs[0:1] - top)
    row = lax.broadcasted_iota(jnp.int32, mine.shape, 0)
    return jnp.where(row == 0, top, sums)


def log_add(one, two):
    return jnp.maximum(one, two) + jnp.log2(1.0 + jnp.exp2(-jnp.abs(one - two)))


def per_device(src_points, tgt_points, log_a, log_b, g_init):
    place = lax.axis_index("tgt")
    share = src_points.shape[1] // lax.axis_size("tgt")
    crossed = (place ^ (place >> 2) ^ (place >> 3)) & 1
    flag = crossed[None]
    with jax.named_scope("cross"):
        other_points = swap(src_points, 1, 0)
        other_a = swap(log_a, 1, 0)
    with jax.named_scope("gather_points_1"):
        more = swap(tgt_points, 1, Z_MASKS[0])
    with jax.named_scope("row_lse"):
        level = row_lse(flag, src_points, other_points, tgt_points, g_init[None, :])[0]
        more, level, other_a, tgt_mass, own_points = lax.optimization_barrier(
            (more, level, other_a, log_b, src_points)
        )
        near = jnp.concatenate([tgt_points, more], 1)
        src_mass = LOG2E * jnp.where(crossed == 1, other_a, log_a)
        tgt_mass = LOG2E * tgt_mass
        picks = [
            lax.dynamic_slice_in_dim(own_points, (place ^ k) * share, share, 1)
            for k in (0, 1, 3, 2)
        ]
        part = jnp.concatenate(picks, 1)
    with jax.named_scope("row_combine"):
        y2, y3 = swap(level, 0, 2), swap(level, 1, 3)
        y1 = swap(level, 1, 1)
        level = log_add(log_add(y2, y3), log_add(level, y1))
        for mask in T_MASKS:
            if mask == T_MASKS[-1]:
                near, level = lax.optimization_barrier((near, level))
            level = log_add(level, swap(level, 1, mask))
        src_term = src_mass - level
    with jax.named_scope("gather_points_2"):
        src_term, tgt_mass = lax.optimization_barrier((src_term, tgt_mass))
        more = swap(near, 1, Z_MASKS[1])
    with jax.named_scope("column_sums"):
        columns = weighted_sums(
            flag, [src_points, other_points], [src_term[None, :]], tgt_points
        )
        columns, more, level, own_points, own_targets = lax.optimization_barrier(
            (columns, more, level, src_points, tgt_points)
        )
        near = jnp.concatenate([near, more], 1)
    with jax.named_scope("column_combine"):
        columns = merge(columns, swap(columns, SRC_MASKS[0], 0))
        columns, near, level = lax.optimization_barrier((columns, near, level))
        for mask in SRC_MASKS[1:]:
            columns = merge(columns, swap(columns, mask, 0))
        tgt_term = tgt_mass - columns[0] - jnp.log2(columns[1])
    with jax.named_scope("gather_points_3"):
        far = swap(near, 1, Z_MASKS[2])
    with jax.named_scope("row_results"):
        level = jnp.where(crossed == 1, swap(level, 1, 0), level)
        f_new = ENTROPY * LN2 * (LOG2E * log_a - level) + jnp.sum(own_points * own_points, 0)

    with jax.named_scope("gather_term"):
        term = tgt_term[None, :]
        term = jnp.concatenate([term, swap(term, 1, Z_MASKS[0])], 1)
        term, tgt_term = lax.optimization_barrier((term, tgt_term))
        term = jnp.concatenate([term, swap(term, 1, Z_MASKS[1])], 1)
        far_term = swap(term, 1, Z_MASKS[2])
    with jax.named_scope("column_results"):
        g_new = ENTROPY * LN2 * tgt_term + jnp.sum(own_targets * own_targets, 0)
        tgt_map = columns[8:24] / columns[1:2]
    with jax.named_scope("row_sums"):
        half = 2 * share
        rows = weighted_sums(flag, [near], [term], part[:, half:])
        rows, far = lax.optimization_barrier((rows, far))
    with jax.named_scope("map_combine"):
        away = merge(rows, weighted_sums(flag, [far], [far_term], part[:, half:]))
        away, far_term = lax.optimization_barrier((away, far_term))
        away = swap(away, 0, 3)
        side = weighted_sums(flag, [near, far], [term, far_term], part[:, share:half])
        side = merge(away[:, share:], side)
        side, far_term = lax.optimization_barrier((side, far_term))
        side = swap(side, 0, 1)
        mine = weighted_sums(flag, [near, far], [term, far_term], part[:, :share])
        rows = merge(merge(away[:, :share], side), mine)
        src_map = rows[8:24] / rows[1:2]
    return (f_new, g_new, src_map, tgt_map)


def solution(mesh):
    in_specs = (P(None, "src"), P(None, "tgt"), P("src"), P("tgt"), P("tgt"))
    out_specs = (P("src"), P("tgt"), P(None, ("src", "tgt")), P(None, "tgt"))
    return jax.shard_map(
        per_device, mesh=mesh, in_specs=in_specs, out_specs=out_specs, check_vma=False
    )
```

```python
import functools
import math

import jax
import jax.numpy as jnp
from jax import lax
from jax.experimental import pallas as pl
from jax.experimental.pallas import tpu as pltpu
from jax.sharding import PartitionSpec as P

LOG2E = math.log2(math.e)
LN2 = math.log(2.0)
ENTROPY = 4.0
ALPHA = LOG2E / ENTROPY
ROWS = 1024
LANES = 256
WIDE = 1024
HEAD = 128
DEPTH = 128
LOWEST = -1e30
bf16 = jnp.bfloat16
f32 = jnp.float32

T_MASKS = (4, 8, 24)
Z_MASKS = (8, 24, 4)
SRC_MASKS = (1, 3, 7)


def split3(values):
    first = values.astype(bf16).astype(f32)
    rest = values - first
    second = rest.astype(bf16).astype(f32)
    third = (rest - second).astype(bf16).astype(f32)
    return first, second, third


def stack_terms(points, potential):
    n = points.shape[1]
    a, b, c = split3(points)
    u, v, w = split3(potential)
    row = lax.broadcasted_iota(jnp.int32, (16, n), 0)
    extra = jnp.where(row == 0, u, jnp.where(row == 1, v, jnp.where(row == 2, w, 0.0)))
    return jnp.concatenate([a, b, c, a, b, a, extra, jnp.zeros((16, n), f32)], 0)


def stack_plain(points):
    n = points.shape[1]
    a, b, c = (part.astype(bf16) for part in split3(points))
    ones = jnp.ones((16, n), bf16)
    return jnp.concatenate([a, a, a, b, b, c, ones, jnp.zeros((16, n), bf16)], 0)


def column_max(x_ref, rows):
    peak = x_ref[0:16, :]
    for at in range(16, rows, 16):
        peak = jnp.maximum(peak, x_ref[at : at + 16, :])
    return jnp.max(peak, axis=0, keepdims=True)


def lse_kernel(
    flag_ref, own_ref, other_ref, tgt_ref, g_ref, out_ref, rows_ref, cols_ref, x0_ref, x1_ref, sum_ref
):
    tgt = tgt_ref[...]
    term = ALPHA * (g_ref[...] - jnp.sum(tgt * tgt, axis=0, keepdims=True))
    rows_ref[...] = stack_terms(tgt, term).T.astype(bf16)
    src = jnp.where(flag_ref[0] != 0, other_ref[...], own_ref[...])
    cols_ref[...] = stack_plain(src * (2.0 * ALPHA))
    tiles = own_ref.shape[1] // WIDE
    slots = (x0_ref, x1_ref)

    def product(tile, x_ref, wide):
        at = pl.multiple_of(tile * wide, wide)
        x_ref[:, :wide] = jnp.dot(
            rows_ref[...], cols_ref[:, pl.ds(at, wide)], preferred_element_type=f32
        )

    def reduce(tile, x_ref, wide, depth):
        at = pl.multiple_of(tile * wide, wide)
        shift = column_max(x_ref.at[:, :wide], depth)
        total = jnp.zeros((16, wide), f32)
        for i in range(0, ROWS, 16):
            total = total + jnp.exp2(x_ref[i : i + 16, :wide] - shift)
        total = jnp.sum(total, axis=0, keepdims=True)
        out_ref[:, pl.ds(at, wide)] = shift + jnp.log2(total)
        sum_ref[:, pl.ds(at, wide)] = total

    product(0, x0_ref, WIDE)

    def body(pair, carry):
        for slot in range(2):
            tile = pair * 2 + slot
            product(jnp.minimum(tile + 1, tiles - 1), slots[1 - slot], WIDE)
            reduce(tile, slots[slot], WIDE, HEAD)
        return carry

    lax.fori_loop(0, tiles // 2, body, 0)

    def again(tile, carry):
        product(tile, x0_ref, LANES)
        reduce(tile, x0_ref, LANES, ROWS)
        return carry

    @pl.when(jnp.logical_not(jnp.max(sum_ref[...]) < 2.0**100))
    def _():
        lax.fori_loop(0, tiles * WIDE // LANES, again, 0)


def two_parts(points):
    first = points.astype(bf16)
    second = (points - first.astype(f32)).astype(bf16)
    return jnp.concatenate([first, jnp.ones(points.shape, bf16), second], 0)


def sums_kernel(arrays, picked, flag_ref, *refs):
    rows_in = refs[: arrays + picked]
    terms = refs[arrays + picked : 2 * arrays + picked]
    cols_in_ref, out_ref, r0_ref, r1_ref, b0_ref, b1_ref, cols_ref, x0_ref, x1_ref, high_ref = refs[
        2 * arrays + picked :
    ]
    each = rows_in[0].shape[1] // ROWS
    blocks = each * arrays
    width = cols_in_ref.shape[1]
    tiles = width // LANES
    unrolled = blocks * tiles <= 8
    sides = (r0_ref, r1_ref)
    boths = (b0_ref, b1_ref)
    slots = (x0_ref, x1_ref)
    cols_ref[...] = stack_plain(cols_in_ref[...] * (2.0 * ALPHA))

    def load(block, first, last, array=None):
        if array is None:
            array = block // each if arrays > 1 else 0
            block = block - array * each
        at = block * ROWS + first
        if not isinstance(at, int):
            at = pl.multiple_of(at, LANES)
        where = pl.ds(at, last - first)
        points = rows_in[array][:, where]
        if picked:
            points = jnp.where(flag_ref[0] != 0, rows_in[1][:, where], points)
        return points, terms[array][:, where]

    def build_side(block, side, first, last):
        points, term = load(block, first, last)
        sides[side][first:last, :] = stack_terms(points, term).T.astype(bf16)

    def build_both(block, side, first, last):
        boths[side][:, first:last] = two_parts(load(block, first, last)[0])

    def product(side, tile, x_ref):
        x_ref[...] = jnp.dot(
            sides[side][...],
            cols_ref[:, tile * LANES : (tile + 1) * LANES],
            preferred_element_type=f32,
        )

    def accumulate(side, here, x_ref, depth):
        shift = column_max(x_ref, depth)
        big = jnp.zeros((48, LANES), f32)
        small = jnp.zeros((32, LANES), f32)
        for at in range(0, ROWS, 256):
            weights = jnp.exp2(x_ref[at : at + 256, :] - shift)
            hi = weights.astype(bf16)
            lo = (weights - hi.astype(f32)).astype(bf16)
            both = boths[side][:, at : at + 256]
            big += jnp.dot(both, hi, preferred_element_type=f32)
            small += jnp.dot(both[0:32], lo, preferred_element_type=f32)
        high_ref[...] = jnp.maximum(high_ref[...], big[16:24])
        before = out_ref[0:1, here]
        after = jnp.maximum(before, shift)
        old = jnp.exp2(before - after)
        new = jnp.exp2(shift - after)
        total = out_ref[0:8, here] * old + (big[16:24] + small[16:24]) * new
        row = lax.broadcasted_iota(jnp.int32, (8, LANES), 0)
        out_ref[0:8, here] = jnp.where(row == 0, after, total)
        mass = big[0:16] + big[32:48] + small[0:16]
        out_ref[8:24, here] = out_ref[8:24, here] * old + mass * new

    def clear():
        row = lax.broadcasted_iota(jnp.int32, (24, width), 0)
        out_ref[...] = jnp.where(row == 0, LOWEST, 0.0)
        high_ref[...] = jnp.zeros((8, LANES), f32)

    def run():
        build_side(0, 0, 0, ROWS)
        build_both(0, 0, 0, ROWS)
        product(0, 0, x0_ref)
        if tiles == 1:
            build_side(1, 1, 0, ROWS)

        def body(pair, carry):
            for step in range(2 * tiles):
                side, tile = divmod(step, tiles)
                block = pair * 2 + side
                later = slots[(step + 1) % 2]
                if isinstance(block, int):
                    after, second = min(block + 1, blocks - 1), min(block + 2, blocks - 1)
                    final = block == blocks - 1
                else:
                    after, final = jnp.minimum(block + 1, blocks - 1), False
                if not final:
                    if tiles == 1:
                        build_both(after, 1 - side, 0, ROWS)
                    elif tile < 2 and tiles > 2:
                        first, last = tile * ROWS // 2, (tile + 1) * ROWS // 2
                        build_side(after, 1 - side, first, last)
                        build_both(after, 1 - side, first, last)
                    elif tile == 0:
                        build_side(after, 1 - side, 0, ROWS)
                        build_both(after, 1 - side, 0, ROWS)
                if tile + 1 < tiles:
                    product(side, tile + 1, later)
                elif not final:
                    product(1 - side, 0, later)
                    if tiles == 1 and block + 2 < blocks:
                        build_side(second, side, 0, ROWS)
                here = slice(tile * LANES, (tile + 1) * LANES)
                accumulate(side, here, slots[step % 2], HEAD)
            return carry

        if unrolled:
            for pair in range(blocks // 2):
                body(pair, 0)
        else:
            lax.fori_loop(0, blocks // 2, body, 0)

    def again(array):
        def body(step, carry):
            block, tile = step // tiles, step % tiles
            here = pl.ds(pl.multiple_of(tile * LANES, LANES), LANES)
            points, term = load(block, 0, ROWS, array)
            r0_ref[...] = stack_terms(points, term).T.astype(bf16)
            b0_ref[...] = two_parts(points)
            x0_ref[...] = jnp.dot(r0_ref[...], cols_ref[:, here], preferred_element_type=f32)
            accumulate(0, here, x0_ref, ROWS)
            return carry

        lax.fori_loop(0, each * tiles, body, 0)

    clear()
    run()

    @pl.when(jnp.logical_not(jnp.max(high_ref[...]) < 2.0**60))
    def _():
        clear()
        for array in range(arrays):
            again(array)


params = pltpu.CompilerParams(vmem_limit_bytes=48 * 1024 * 1024)
vmem = pl.BlockSpec(memory_space=pltpu.VMEM)
scalars = pl.BlockSpec(memory_space=pltpu.SMEM)


def cost(rows, columns):
    pairs = rows * columns
    return pl.CostEstimate(
        flops=1500 * pairs, transcendentals=pairs, bytes_accessed=64 * (rows + columns)
    )


def row_lse(flag, own, other, tgt, g):
    n, k = own.shape[1], tgt.shape[1]
    return pl.pallas_call(
        lse_kernel,
        out_shape=jax.ShapeDtypeStruct((1, n), f32),
        in_specs=[scalars] + [vmem] * 4,
        out_specs=vmem,
        scratch_shapes=[
            pltpu.VMEM((k, DEPTH), bf16),
            pltpu.VMEM((DEPTH, n), bf16),
            pltpu.VMEM((ROWS, WIDE), f32),
            pltpu.VMEM((ROWS, WIDE), f32),
            pltpu.VMEM((1, n), f32),
        ],
        compiler_params=params,
        cost_estimate=cost(n, k),
        name="row_lse",
    )(flag, own, other, tgt, g)


def weighted_sums(flag, rows, terms, columns):
    n, k = rows[0].shape[1], columns.shape[1]
    arrays, picked = len(terms), len(rows) - len(terms)
    return pl.pallas_call(
        functools.partial(sums_kernel, arrays, picked),
        out_shape=jax.ShapeDtypeStruct((24, k), f32),
        in_specs=[scalars] + [vmem] * (len(rows) + len(terms) + 1),
        out_specs=vmem,
        scratch_shapes=[
            pltpu.VMEM((ROWS, DEPTH), bf16),
            pltpu.VMEM((ROWS, DEPTH), bf16),
            pltpu.VMEM((48, ROWS), bf16),
            pltpu.VMEM((48, ROWS), bf16),
            pltpu.VMEM((DEPTH, k), bf16),
            pltpu.VMEM((ROWS, LANES), f32),
            pltpu.VMEM((ROWS, LANES), f32),
            pltpu.VMEM((8, LANES), f32),
        ],
        compiler_params=params,
        cost_estimate=cost(n * arrays, k),
        name="weighted_sums",
    )(flag, *rows, *terms, columns)


def swap(values, src_mask, tgt_mask):
    width = lax.axis_size("tgt")
    size = width * lax.axis_size("src")
    mask = src_mask * width + tgt_mask
    return lax.ppermute(values, ("src", "tgt"), [(i, i ^ mask) for i in range(size)])


def merge(mine, theirs):
    top = jnp.maximum(mine[0:1], theirs[0:1])
    sums = mine * jnp.exp2(mine[0:1] - top) + theirs * jnp.exp2(theirs[0:1] - top)
    row = lax.broadcasted_iota(jnp.int32, mine.shape, 0)
    return jnp.where(row == 0, top, sums)


def log_add(one, two):
    return jnp.maximum(one, two) + jnp.log2(1.0 + jnp.exp2(-jnp.abs(one - two)))


def per_device(src_points, tgt_points, log_a, log_b, g_init):
    place = lax.axis_index("tgt")
    share = src_points.shape[1] // lax.axis_size("tgt")
    crossed = (place ^ (place >> 2) ^ (place >> 3)) & 1
    flag = crossed[None]
    with jax.named_scope("cross"):
        other_points = swap(src_points, 1, 0)
        other_a = swap(log_a, 1, 0)
    with jax.named_scope("gather_points_1"):
        more = swap(tgt_points, 1, Z_MASKS[0])
    with jax.named_scope("row_lse"):
        level = row_lse(flag, src_points, other_points, tgt_points, g_init[None, :])[0]
        more, level, other_a, tgt_mass, own_points = lax.optimization_barrier(
            (more, level, other_a, log_b, src_points)
        )
        near = jnp.concatenate([tgt_points, more], 1)
        src_mass = LOG2E * jnp.where(crossed == 1, other_a, log_a)
        tgt_mass = LOG2E * tgt_mass
        picks = [
            lax.dynamic_slice_in_dim(own_points, (place ^ k) * share, share, 1)
            for k in (0, 1, 3, 2)
        ]
        part = jnp.concatenate(picks, 1)
    with jax.named_scope("row_combine"):
        y2, y3 = swap(level, 0, 2), swap(level, 1, 3)
        y1 = swap(level, 1, 1)
        level = log_add(log_add(y2, y3), log_add(level, y1))
        for mask in T_MASKS:
            if mask == T_MASKS[-1]:
                near, level = lax.optimization_barrier((near, level))
            level = log_add(level, swap(level, 1, mask))
        src_term = src_mass - level
    with jax.named_scope("gather_points_2"):
        src_term, tgt_mass = lax.optimization_barrier((src_term, tgt_mass))
        more = swap(near, 1, Z_MASKS[1])
    with jax.named_scope("column_sums"):
        columns = weighted_sums(
            flag, [src_points, other_points], [src_term[None, :]], tgt_points
        )
        columns, more, level, own_points, own_targets = lax.optimization_barrier(
            (columns, more, level, src_points, tgt_points)
        )
        near = jnp.concatenate([near, more], 1)
    with jax.named_scope("column_combine"):
        columns = merge(columns, swap(columns, SRC_MASKS[0], 0))
        columns, near, level = lax.optimization_barrier((columns, near, level))
        for mask in SRC_MASKS[1:]:
            columns = merge(columns, swap(columns, mask, 0))
        tgt_term = tgt_mass - columns[0] - jnp.log2(columns[1])
    with jax.named_scope("gather_points_3"):
        far = swap(near, 1, Z_MASKS[2])
    with jax.named_scope("row_results"):
        level = jnp.where(crossed == 1, swap(level, 1, 0), level)
        f_new = ENTROPY * LN2 * (LOG2E * log_a - level) + jnp.sum(own_points * own_points, 0)

    with jax.named_scope("gather_term"):
        term = tgt_term[None, :]
        term = jnp.concatenate([term, swap(term, 1, Z_MASKS[0])], 1)
        term, tgt_term = lax.optimization_barrier((term, tgt_term))
        term = jnp.concatenate([term, swap(term, 1, Z_MASKS[1])], 1)
        far_term = swap(term, 1, Z_MASKS[2])
    with jax.named_scope("column_results"):
        g_new = ENTROPY * LN2 * tgt_term + jnp.sum(own_targets * own_targets, 0)
        tgt_map = columns[8:24] / columns[1:2]
    with jax.named_scope("row_sums"):
        half = 2 * share
        rows = weighted_sums(flag, [near], [term], part[:, half:])
        rows, far = lax.optimization_barrier((rows, far))
    with jax.named_scope("map_combine"):
        away = merge(rows, weighted_sums(flag, [far], [far_term], part[:, half:]))
        away, far_term = lax.optimization_barrier((away, far_term))
        away = swap(away, 0, 3)
        side = weighted_sums(flag, [near, far], [term, far_term], part[:, share:half])
        side = merge(away[:, share:], side)
        side, far_term = lax.optimization_barrier((side, far_term))
        side = swap(side, 0, 1)
        mine = weighted_sums(flag, [near, far], [term, far_term], part[:, :share])
        rows = merge(merge(away[:, :share], side), mine)
        src_map = rows[8:24] / rows[1:2]
    return (f_new, g_new, src_map, tgt_map)


def solution(mesh):
    in_specs = (P(None, "src"), P(None, "tgt"), P("src"), P("tgt"), P("tgt"))
    out_specs = (P("src"), P("tgt"), P(None, ("src", "tgt")), P(None, "tgt"))
    return jax.shard_map(
        per_device, mesh=mesh, in_specs=in_specs, out_specs=out_specs, check_vma=False
    )
```

```python
import functools
import math

import jax
import jax.numpy as jnp
from jax import lax
from jax.experimental import pallas as pl
from jax.experimental.pallas import tpu as pltpu
from jax.sharding import PartitionSpec as P

LOG2E = math.log2(math.e)
LN2 = math.log(2.0)
ENTROPY = 4.0
ALPHA = LOG2E / ENTROPY
ROWS = 1024
LANES = 256
WIDE = 1024
HEAD = 128
DEPTH = 128
LOWEST = -1e30
bf16 = jnp.bfloat16
f32 = jnp.float32

T_MASKS = (4, 8, 24)
Z_MASKS = (8, 24, 4)
SRC_MASKS = (1, 3, 7)


def split3(values):
    first = values.astype(bf16).astype(f32)
    rest = values - first
    second = rest.astype(bf16).astype(f32)
    third = (rest - second).astype(bf16).astype(f32)
    return first, second, third


def stack_terms(points, potential):
    n = points.shape[1]
    a, b, c = split3(points)
    u, v, w = split3(potential)
    row = lax.broadcasted_iota(jnp.int32, (16, n), 0)
    extra = jnp.where(row == 0, u, jnp.where(row == 1, v, jnp.where(row == 2, w, 0.0)))
    return jnp.concatenate([a, b, c, a, b, a, extra, jnp.zeros((16, n), f32)], 0)


def stack_plain(points):
    n = points.shape[1]
    a, b, c = (part.astype(bf16) for part in split3(points))
    ones = jnp.ones((16, n), bf16)
    return jnp.concatenate([a, a, a, b, b, c, ones, jnp.zeros((16, n), bf16)], 0)


def column_max(x_ref, rows):
    peak = x_ref[0:16, :]
    for at in range(16, rows, 16):
        peak = jnp.maximum(peak, x_ref[at : at + 16, :])
    return jnp.max(peak, axis=0, keepdims=True)


def lse_kernel(
    flag_ref, own_ref, other_ref, tgt_ref, g_ref, out_ref, rows_ref, cols_ref, x0_ref, x1_ref, sum_ref
):
    tgt = tgt_ref[...]
    term = ALPHA * (g_ref[...] - jnp.sum(tgt * tgt, axis=0, keepdims=True))
    rows_ref[...] = stack_terms(tgt, term).T.astype(bf16)
    src = jnp.where(flag_ref[0] != 0, other_ref[...], own_ref[...])
    cols_ref[...] = stack_plain(src * (2.0 * ALPHA))
    tiles = own_ref.shape[1] // WIDE
    slots = (x0_ref, x1_ref)

    def product(tile, x_ref, wide):
        at = pl.multiple_of(tile * wide, wide)
        x_ref[:, :wide] = jnp.dot(
            rows_ref[...], cols_ref[:, pl.ds(at, wide)], preferred_element_type=f32
        )

    def reduce(tile, x_ref, wide, depth):
        at = pl.multiple_of(tile * wide, wide)
        shift = column_max(x_ref.at[:, :wide], depth)
        total = jnp.zeros((16, wide), f32)
        for i in range(0, ROWS, 16):
            total = total + jnp.exp2(x_ref[i : i + 16, :wide] - shift)
        total = jnp.sum(total, axis=0, keepdims=True)
        out_ref[:, pl.ds(at, wide)] = shift + jnp.log2(total)
        sum_ref[:, pl.ds(at, wide)] = total

    product(0, x0_ref, WIDE)

    def body(pair, carry):
        for slot in range(2):
            tile = pair * 2 + slot
            product(jnp.minimum(tile + 1, tiles - 1), slots[1 - slot], WIDE)
            reduce(tile, slots[slot], WIDE, HEAD)
        return carry

    lax.fori_loop(0, tiles // 2, body, 0)

    def again(tile, carry):
        product(tile, x0_ref, LANES)
        reduce(tile, x0_ref, LANES, ROWS)
        return carry

    @pl.when(jnp.logical_not(jnp.max(sum_ref[...]) < 2.0**100))
    def _():
        lax.fori_loop(0, tiles * WIDE // LANES, again, 0)


def two_parts(points):
    first = points.astype(bf16)
    second = (points - first.astype(f32)).astype(bf16)
    return jnp.concatenate([first, jnp.ones(points.shape, bf16), second], 0)


def sums_kernel(arrays, picked, flag_ref, *refs):
    rows_in = refs[: arrays + picked]
    terms = refs[arrays + picked : 2 * arrays + picked]
    cols_in_ref, out_ref, r0_ref, r1_ref, b0_ref, b1_ref, cols_ref, x0_ref, x1_ref, high_ref = refs[
        2 * arrays + picked :
    ]
    each = rows_in[0].shape[1] // ROWS
    blocks = each * arrays
    width = cols_in_ref.shape[1]
    tiles = width // LANES
    unrolled = blocks * tiles <= 8
    sides = (r0_ref, r1_ref)
    boths = (b0_ref, b1_ref)
    slots = (x0_ref, x1_ref)
    cols_ref[...] = stack_plain(cols_in_ref[...] * (2.0 * ALPHA))

    def load(block, first, last, array=None):
        if array is None:
            array = block // each if arrays > 1 else 0
            block = block - array * each
        at = block * ROWS + first
        if not isinstance(at, int):
            at = pl.multiple_of(at, LANES)
        where = pl.ds(at, last - first)
        points = rows_in[array][:, where]
        if picked:
            points = jnp.where(flag_ref[0] != 0, rows_in[1][:, where], points)
        return points, terms[array][:, where]

    def build_side(block, side, first, last):
        points, term = load(block, first, last)
        sides[side][first:last, :] = stack_terms(points, term).T.astype(bf16)

    def build_both(block, side, first, last):
        boths[side][:, first:last] = two_parts(load(block, first, last)[0])

    def product(side, tile, x_ref):
        x_ref[...] = jnp.dot(
            sides[side][...],
            cols_ref[:, tile * LANES : (tile + 1) * LANES],
            preferred_element_type=f32,
        )

    def accumulate(side, here, x_ref, depth):
        shift = column_max(x_ref, depth)
        big = jnp.zeros((48, LANES), f32)
        small = jnp.zeros((32, LANES), f32)
        for at in range(0, ROWS, 256):
            weights = jnp.exp2(x_ref[at : at + 256, :] - shift)
            hi = weights.astype(bf16)
            lo = (weights - hi.astype(f32)).astype(bf16)
            both = boths[side][:, at : at + 256]
            big += jnp.dot(both, hi, preferred_element_type=f32)
            small += jnp.dot(both[0:32], lo, preferred_element_type=f32)
        high_ref[...] = jnp.maximum(high_ref[...], big[16:24])
        before = out_ref[0:1, here]
        after = jnp.maximum(before, shift)
        old = jnp.exp2(before - after)
        new = jnp.exp2(shift - after)
        total = out_ref[0:8, here] * old + (big[16:24] + small[16:24]) * new
        row = lax.broadcasted_iota(jnp.int32, (8, LANES), 0)
        out_ref[0:8, here] = jnp.where(row == 0, after, total)
        mass = big[0:16] + big[32:48] + small[0:16]
        out_ref[8:24, here] = out_ref[8:24, here] * old + mass * new

    def clear():
        row = lax.broadcasted_iota(jnp.int32, (24, width), 0)
        out_ref[...] = jnp.where(row == 0, LOWEST, 0.0)
        high_ref[...] = jnp.zeros((8, LANES), f32)

    def run():
        build_side(0, 0, 0, ROWS)
        build_both(0, 0, 0, ROWS)
        product(0, 0, x0_ref)
        if tiles == 1:
            build_side(1, 1, 0, ROWS)

        def body(pair, carry):
            for step in range(2 * tiles):
                side, tile = divmod(step, tiles)
                block = pair * 2 + side
                later = slots[(step + 1) % 2]
                if isinstance(block, int):
                    after, second = min(block + 1, blocks - 1), min(block + 2, blocks - 1)
                    final = block == blocks - 1
                else:
                    after, final = jnp.minimum(block + 1, blocks - 1), False
                if not final:
                    if tiles == 1:
                        build_both(after, 1 - side, 0, ROWS)
                    elif tile < 2 and tiles > 2:
                        first, last = tile * ROWS // 2, (tile + 1) * ROWS // 2
                        build_side(after, 1 - side, first, last)
                        build_both(after, 1 - side, first, last)
                    elif tile == 0:
                        build_side(after, 1 - side, 0, ROWS)
                        build_both(after, 1 - side, 0, ROWS)
                if tile + 1 < tiles:
                    product(side, tile + 1, later)
                elif not final:
                    product(1 - side, 0, later)
                    if tiles == 1 and block + 2 < blocks:
                        build_side(second, side, 0, ROWS)
                here = slice(tile * LANES, (tile + 1) * LANES)
                accumulate(side, here, slots[step % 2], HEAD)
            return carry

        if unrolled:
            for pair in range(blocks // 2):
                body(pair, 0)
        else:
            lax.fori_loop(0, blocks // 2, body, 0)

    def again(array):
        def body(step, carry):
            block, tile = step // tiles, step % tiles
            here = pl.ds(pl.multiple_of(tile * LANES, LANES), LANES)
            points, term = load(block, 0, ROWS, array)
            r0_ref[...] = stack_terms(points, term).T.astype(bf16)
            b0_ref[...] = two_parts(points)
            x0_ref[...] = jnp.dot(r0_ref[...], cols_ref[:, here], preferred_element_type=f32)
            accumulate(0, here, x0_ref, ROWS)
            return carry

        lax.fori_loop(0, each * tiles, body, 0)

    clear()
    run()

    @pl.when(jnp.logical_not(jnp.max(high_ref[...]) < 2.0**60))
    def _():
        clear()
        for array in range(arrays):
            again(array)


params = pltpu.CompilerParams(vmem_limit_bytes=48 * 1024 * 1024)
vmem = pl.BlockSpec(memory_space=pltpu.VMEM)
scalars = pl.BlockSpec(memory_space=pltpu.SMEM)


def cost(rows, columns):
    pairs = rows * columns
    return pl.CostEstimate(
        flops=1500 * pairs, transcendentals=pairs, bytes_accessed=64 * (rows + columns)
    )


def row_lse(flag, own, other, tgt, g):
    n, k = own.shape[1], tgt.shape[1]
    return pl.pallas_call(
        lse_kernel,
        out_shape=jax.ShapeDtypeStruct((1, n), f32),
        in_specs=[scalars] + [vmem] * 4,
        out_specs=vmem,
        scratch_shapes=[
            pltpu.VMEM((k, DEPTH), bf16),
            pltpu.VMEM((DEPTH, n), bf16),
            pltpu.VMEM((ROWS, WIDE), f32),
            pltpu.VMEM((ROWS, WIDE), f32),
            pltpu.VMEM((1, n), f32),
        ],
        compiler_params=params,
        cost_estimate=cost(n, k),
        name="row_lse",
    )(flag, own, other, tgt, g)


def weighted_sums(flag, rows, terms, columns):
    n, k = rows[0].shape[1], columns.shape[1]
    arrays, picked = len(terms), len(rows) - len(terms)
    return pl.pallas_call(
        functools.partial(sums_kernel, arrays, picked),
        out_shape=jax.ShapeDtypeStruct((24, k), f32),
        in_specs=[scalars] + [vmem] * (len(rows) + len(terms) + 1),
        out_specs=vmem,
        scratch_shapes=[
            pltpu.VMEM((ROWS, DEPTH), bf16),
            pltpu.VMEM((ROWS, DEPTH), bf16),
            pltpu.VMEM((48, ROWS), bf16),
            pltpu.VMEM((48, ROWS), bf16),
            pltpu.VMEM((DEPTH, k), bf16),
            pltpu.VMEM((ROWS, LANES), f32),
            pltpu.VMEM((ROWS, LANES), f32),
            pltpu.VMEM((8, LANES), f32),
        ],
        compiler_params=params,
        cost_estimate=cost(n * arrays, k),
        name="weighted_sums",
    )(flag, *rows, *terms, columns)


def swap(values, src_mask, tgt_mask):
    width = lax.axis_size("tgt")
    size = width * lax.axis_size("src")
    mask = src_mask * width + tgt_mask
    return lax.ppermute(values, ("src", "tgt"), [(i, i ^ mask) for i in range(size)])


def merge(mine, theirs):
    top = jnp.maximum(mine[0:1], theirs[0:1])
    sums = mine * jnp.exp2(mine[0:1] - top) + theirs * jnp.exp2(theirs[0:1] - top)
    row = lax.broadcasted_iota(jnp.int32, mine.shape, 0)
    return jnp.where(row == 0, top, sums)


def log_add(one, two):
    return jnp.maximum(one, two) + jnp.log2(1.0 + jnp.exp2(-jnp.abs(one - two)))


def per_device(src_points, tgt_points, log_a, log_b, g_init):
    place = lax.axis_index("tgt")
    share = src_points.shape[1] // lax.axis_size("tgt")
    crossed = (place ^ (place >> 2) ^ (place >> 3)) & 1
    flag = crossed[None]
    with jax.named_scope("cross"):
        other_points = swap(src_points, 1, 0)
        other_a = swap(log_a, 1, 0)
    with jax.named_scope("gather_points_1"):
        more = swap(tgt_points, 1, Z_MASKS[0])
    with jax.named_scope("row_lse"):
        level = row_lse(flag, src_points, other_points, tgt_points, g_init[None, :])[0]
        more, level, other_a, tgt_mass, own_points = lax.optimization_barrier(
            (more, level, other_a, log_b, src_points)
        )
        near = jnp.concatenate([tgt_points, more], 1)
        src_mass = LOG2E * jnp.where(crossed == 1, other_a, log_a)
        tgt_mass = LOG2E * tgt_mass
        picks = [
            lax.dynamic_slice_in_dim(own_points, (place ^ k) * share, share, 1)
            for k in (0, 1, 3, 2)
        ]
        part = jnp.concatenate(picks, 1)
    with jax.named_scope("row_combine"):
        y2, y3 = swap(level, 0, 2), swap(level, 1, 3)
        y1 = swap(level, 1, 1)
        level = log_add(log_add(y2, y3), log_add(level, y1))
        for mask in T_MASKS:
            if mask == T_MASKS[-1]:
                near, level = lax.optimization_barrier((near, level))
            level = log_add(level, swap(level, 1, mask))
        src_term = src_mass - level
    with jax.named_scope("gather_points_2"):
        src_term, tgt_mass = lax.optimization_barrier((src_term, tgt_mass))
        more = swap(near, 1, Z_MASKS[1])
    with jax.named_scope("column_sums"):
        columns = weighted_sums(
            flag, [src_points, other_points], [src_term[None, :]], tgt_points
        )
        columns, more, level, own_points, own_targets = lax.optimization_barrier(
            (columns, more, level, src_points, tgt_points)
        )
        near = jnp.concatenate([near, more], 1)
    with jax.named_scope("column_combine"):
        columns = merge(columns, swap(columns, SRC_MASKS[0], 0))
        member = lax.axis_index("src")
        upper = (member ^ (member >> 1)) & 1 == 1
        columns = jnp.concatenate(
            [columns[0:8], jnp.where(upper, columns[16:24], columns[8:16])], 0
        )
        columns, near, level = lax.optimization_barrier((columns, near, level))
        for mask in SRC_MASKS[1:]:
            columns = merge(columns, swap(columns, mask, 0))
        tgt_term = tgt_mass - columns[0] - jnp.log2(columns[1])
    with jax.named_scope("gather_points_3"):
        far = swap(near, 1, Z_MASKS[2])
    with jax.named_scope("row_results"):
        level = jnp.where(crossed == 1, swap(level, 1, 0), level)
        f_new = ENTROPY * LN2 * (LOG2E * log_a - level) + jnp.sum(own_points * own_points, 0)

    with jax.named_scope("gather_term"):
        term = tgt_term[None, :]
        term = jnp.concatenate([term, swap(term, 1, Z_MASKS[0])], 1)
        kept = columns[8:16]
        other = swap(kept, 1, 0)
        term, tgt_term, other, far = lax.optimization_barrier((term, tgt_term, other, far))
        term = jnp.concatenate([term, swap(term, 1, Z_MASKS[1])], 1)
        far_term = swap(term, 1, Z_MASKS[2])
    with jax.named_scope("column_results"):
        g_new = ENTROPY * LN2 * tgt_term + jnp.sum(own_targets * own_targets, 0)
        mass = jnp.concatenate([jnp.where(upper, other, kept), jnp.where(upper, kept, other)], 0)
        tgt_map = mass / columns[1:2]
    with jax.named_scope("row_sums"):
        half = 2 * share
        rows = weighted_sums(flag, [near], [term], part[:, half:])
        rows, far = lax.optimization_barrier((rows, far))
    with jax.named_scope("map_combine"):
        away = merge(rows, weighted_sums(flag, [far], [far_term], part[:, half:]))
        away, far_term = lax.optimization_barrier((away, far_term))
        away = swap(away, 0, 3)
        side = weighted_sums(flag, [near, far], [term, far_term], part[:, share:half])
        side = merge(away[:, share:], side)
        side, far_term = lax.optimization_barrier((side, far_term))
        side = swap(side, 0, 1)
        mine = weighted_sums(flag, [near, far], [term, far_term], part[:, :share])
        rows = merge(merge(away[:, :share], side), mine)
        src_map = rows[8:24] / rows[1:2]
    return (f_new, g_new, src_map, tgt_map)


def solution(mesh):
    in_specs = (P(None, "src"), P(None, "tgt"), P("src"), P("tgt"), P("tgt"))
    out_specs = (P("src"), P("tgt"), P(None, ("src", "tgt")), P(None, "tgt"))
    return jax.shard_map(
        per_device, mesh=mesh, in_specs=in_specs, out_specs=out_specs, check_vma=False
    )
```

```python
import functools
import math

import jax
import jax.numpy as jnp
from jax import lax
from jax.experimental import pallas as pl
from jax.experimental.pallas import tpu as pltpu
from jax.sharding import PartitionSpec as P

LOG2E = math.log2(math.e)
LN2 = math.log(2.0)
ENTROPY = 4.0
ALPHA = LOG2E / ENTROPY
ROWS = 1024
LANES = 256
WIDE = 1024
HEAD = 128
DEPTH = 128
LOWEST = -1e30
bf16 = jnp.bfloat16
f32 = jnp.float32

T_MASKS = (4, 8, 24)
Z_MASKS = (8, 24, 4)
SRC_MASKS = (1, 3, 7)


def split3(values):
    first = values.astype(bf16).astype(f32)
    rest = values - first
    second = rest.astype(bf16).astype(f32)
    third = (rest - second).astype(bf16).astype(f32)
    return first, second, third


def stack_terms(points, potential):
    n = points.shape[1]
    a, b, c = split3(points)
    u, v, w = split3(potential)
    row = lax.broadcasted_iota(jnp.int32, (16, n), 0)
    extra = jnp.where(row == 0, u, jnp.where(row == 1, v, jnp.where(row == 2, w, 0.0)))
    return jnp.concatenate([a, b, c, a, b, a, extra, jnp.zeros((16, n), f32)], 0)


def stack_plain(points):
    n = points.shape[1]
    a, b, c = (part.astype(bf16) for part in split3(points))
    ones = jnp.ones((16, n), bf16)
    return jnp.concatenate([a, a, a, b, b, c, ones, jnp.zeros((16, n), bf16)], 0)


def column_max(x_ref, rows):
    peak = x_ref[0:16, :]
    for at in range(16, rows, 16):
        peak = jnp.maximum(peak, x_ref[at : at + 16, :])
    return jnp.max(peak, axis=0, keepdims=True)


def lse_kernel(
    flag_ref, own_ref, other_ref, tgt_ref, g_ref, out_ref, rows_ref, cols_ref, x0_ref, x1_ref, sum_ref
):
    tgt = tgt_ref[...]
    term = ALPHA * (g_ref[...] - jnp.sum(tgt * tgt, axis=0, keepdims=True))
    rows_ref[...] = stack_terms(tgt, term).T.astype(bf16)
    src = jnp.where(flag_ref[0] != 0, other_ref[...], own_ref[...])
    cols_ref[...] = stack_plain(src * (2.0 * ALPHA))
    tiles = own_ref.shape[1] // WIDE
    slots = (x0_ref, x1_ref)

    def product(tile, x_ref, wide):
        at = pl.multiple_of(tile * wide, wide)
        x_ref[:, :wide] = jnp.dot(
            rows_ref[...], cols_ref[:, pl.ds(at, wide)], preferred_element_type=f32
        )

    def reduce(tile, x_ref, wide, depth):
        at = pl.multiple_of(tile * wide, wide)
        shift = column_max(x_ref.at[:, :wide], depth)
        total = jnp.zeros((16, wide), f32)
        for i in range(0, ROWS, 16):
            total = total + jnp.exp2(x_ref[i : i + 16, :wide] - shift)
        total = jnp.sum(total, axis=0, keepdims=True)
        out_ref[:, pl.ds(at, wide)] = shift + jnp.log2(total)
        sum_ref[:, pl.ds(at, wide)] = total

    product(0, x0_ref, WIDE)

    def body(pair, carry):
        for slot in range(2):
            tile = pair * 2 + slot
            product(jnp.minimum(tile + 1, tiles - 1), slots[1 - slot], WIDE)
            reduce(tile, slots[slot], WIDE, HEAD)
        return carry

    lax.fori_loop(0, tiles // 2, body, 0)

    def again(tile, carry):
        product(tile, x0_ref, LANES)
        reduce(tile, x0_ref, LANES, ROWS)
        return carry

    @pl.when(jnp.logical_not(jnp.max(sum_ref[...]) < 2.0**100))
    def _():
        lax.fori_loop(0, tiles * WIDE // LANES, again, 0)


def two_parts(points):
    first = points.astype(bf16)
    second = (points - first.astype(f32)).astype(bf16)
    return jnp.concatenate([first, jnp.ones(points.shape, bf16), second], 0)


def sums_kernel(arrays, picked, flag_ref, *refs):
    rows_in = refs[: arrays + picked]
    terms = refs[arrays + picked : 2 * arrays + picked]
    cols_in_ref, out_ref, r0_ref, r1_ref, b0_ref, b1_ref, cols_ref, x0_ref, x1_ref, high_ref = refs[
        2 * arrays + picked :
    ]
    each = rows_in[0].shape[1] // ROWS
    blocks = each * arrays
    width = cols_in_ref.shape[1]
    tiles = width // LANES
    unrolled = blocks * tiles <= 8
    sides = (r0_ref, r1_ref)
    boths = (b0_ref, b1_ref)
    slots = (x0_ref, x1_ref)
    cols_ref[...] = stack_plain(cols_in_ref[...] * (2.0 * ALPHA))

    def load(block, first, last, array=None):
        if array is None:
            array = block // each if arrays > 1 else 0
            block = block - array * each
        at = block * ROWS + first
        if not isinstance(at, int):
            at = pl.multiple_of(at, LANES)
        where = pl.ds(at, last - first)
        points = rows_in[array][:, where]
        if picked:
            points = jnp.where(flag_ref[0] != 0, rows_in[1][:, where], points)
        return points, terms[array][:, where]

    def build_side(block, side, first, last):
        points, term = load(block, first, last)
        sides[side][first:last, :] = stack_terms(points, term).T.astype(bf16)

    def build_both(block, side, first, last):
        boths[side][:, first:last] = two_parts(load(block, first, last)[0])

    def product(side, tile, x_ref):
        x_ref[...] = jnp.dot(
            sides[side][...],
            cols_ref[:, tile * LANES : (tile + 1) * LANES],
            preferred_element_type=f32,
        )

    def accumulate(side, here, x_ref, depth):
        shift = column_max(x_ref, depth)
        big = jnp.zeros((48, LANES), f32)
        small = jnp.zeros((32, LANES), f32)
        for at in range(0, ROWS, 256):
            weights = jnp.exp2(x_ref[at : at + 256, :] - shift)
            hi = weights.astype(bf16)
            lo = (weights - hi.astype(f32)).astype(bf16)
            both = boths[side][:, at : at + 256]
            big += jnp.dot(both, hi, preferred_element_type=f32)
            small += jnp.dot(both[0:32], lo, preferred_element_type=f32)
        high_ref[...] = jnp.maximum(high_ref[...], big[16:24])
        before = out_ref[0:1, here]
        after = jnp.maximum(before, shift)
        old = jnp.exp2(before - after)
        new = jnp.exp2(shift - after)
        total = out_ref[0:8, here] * old + (big[16:24] + small[16:24]) * new
        row = lax.broadcasted_iota(jnp.int32, (8, LANES), 0)
        out_ref[0:8, here] = jnp.where(row == 0, after, total)
        mass = big[0:16] + big[32:48] + small[0:16]
        out_ref[8:24, here] = out_ref[8:24, here] * old + mass * new

    def clear():
        row = lax.broadcasted_iota(jnp.int32, (24, width), 0)
        out_ref[...] = jnp.where(row == 0, LOWEST, 0.0)
        high_ref[...] = jnp.zeros((8, LANES), f32)

    def run():
        build_side(0, 0, 0, ROWS)
        build_both(0, 0, 0, ROWS)
        product(0, 0, x0_ref)
        if tiles == 1:
            build_side(1, 1, 0, ROWS)

        def body(pair, carry):
            for step in range(2 * tiles):
                side, tile = divmod(step, tiles)
                block = pair * 2 + side
                later = slots[(step + 1) % 2]
                if isinstance(block, int):
                    after, second = min(block + 1, blocks - 1), min(block + 2, blocks - 1)
                    final = block == blocks - 1
                else:
                    after, final = jnp.minimum(block + 1, blocks - 1), False
                if not final:
                    if tiles == 1:
                        build_both(after, 1 - side, 0, ROWS)
                    elif tile < 2 and tiles > 2:
                        first, last = tile * ROWS // 2, (tile + 1) * ROWS // 2
                        build_side(after, 1 - side, first, last)
                        build_both(after, 1 - side, first, last)
                    elif tile == 0:
                        build_side(after, 1 - side, 0, ROWS)
                        build_both(after, 1 - side, 0, ROWS)
                if tile + 1 < tiles:
                    product(side, tile + 1, later)
                elif not final:
                    product(1 - side, 0, later)
                    if tiles == 1 and block + 2 < blocks:
                        build_side(second, side, 0, ROWS)
                here = slice(tile * LANES, (tile + 1) * LANES)
                accumulate(side, here, slots[step % 2], HEAD)
            return carry

        if unrolled:
            for pair in range(blocks // 2):
                body(pair, 0)
        else:
            lax.fori_loop(0, blocks // 2, body, 0)

    def again(array):
        def body(step, carry):
            block, tile = step // tiles, step % tiles
            here = pl.ds(pl.multiple_of(tile * LANES, LANES), LANES)
            points, term = load(block, 0, ROWS, array)
            r0_ref[...] = stack_terms(points, term).T.astype(bf16)
            b0_ref[...] = two_parts(points)
            x0_ref[...] = jnp.dot(r0_ref[...], cols_ref[:, here], preferred_element_type=f32)
            accumulate(0, here, x0_ref, ROWS)
            return carry

        lax.fori_loop(0, each * tiles, body, 0)

    clear()
    run()

    @pl.when(jnp.logical_not(jnp.max(high_ref[...]) < 2.0**60))
    def _():
        clear()
        for array in range(arrays):
            again(array)


params = pltpu.CompilerParams(vmem_limit_bytes=48 * 1024 * 1024)
vmem = pl.BlockSpec(memory_space=pltpu.VMEM)
scalars = pl.BlockSpec(memory_space=pltpu.SMEM)


def cost(rows, columns):
    pairs = rows * columns
    return pl.CostEstimate(
        flops=1500 * pairs, transcendentals=pairs, bytes_accessed=64 * (rows + columns)
    )


def row_lse(flag, own, other, tgt, g):
    n, k = own.shape[1], tgt.shape[1]
    return pl.pallas_call(
        lse_kernel,
        out_shape=jax.ShapeDtypeStruct((1, n), f32),
        in_specs=[scalars] + [vmem] * 4,
        out_specs=vmem,
        scratch_shapes=[
            pltpu.VMEM((k, DEPTH), bf16),
            pltpu.VMEM((DEPTH, n), bf16),
            pltpu.VMEM((ROWS, WIDE), f32),
            pltpu.VMEM((ROWS, WIDE), f32),
            pltpu.VMEM((1, n), f32),
        ],
        compiler_params=params,
        cost_estimate=cost(n, k),
        name="row_lse",
    )(flag, own, other, tgt, g)


def weighted_sums(flag, rows, terms, columns):
    n, k = rows[0].shape[1], columns.shape[1]
    arrays, picked = len(terms), len(rows) - len(terms)
    return pl.pallas_call(
        functools.partial(sums_kernel, arrays, picked),
        out_shape=jax.ShapeDtypeStruct((24, k), f32),
        in_specs=[scalars] + [vmem] * (len(rows) + len(terms) + 1),
        out_specs=vmem,
        scratch_shapes=[
            pltpu.VMEM((ROWS, DEPTH), bf16),
            pltpu.VMEM((ROWS, DEPTH), bf16),
            pltpu.VMEM((48, ROWS), bf16),
            pltpu.VMEM((48, ROWS), bf16),
            pltpu.VMEM((DEPTH, k), bf16),
            pltpu.VMEM((ROWS, LANES), f32),
            pltpu.VMEM((ROWS, LANES), f32),
            pltpu.VMEM((8, LANES), f32),
        ],
        compiler_params=params,
        cost_estimate=cost(n * arrays, k),
        name="weighted_sums",
    )(flag, *rows, *terms, columns)


def swap(values, src_mask, tgt_mask):
    width = lax.axis_size("tgt")
    size = width * lax.axis_size("src")
    mask = src_mask * width + tgt_mask
    return lax.ppermute(values, ("src", "tgt"), [(i, i ^ mask) for i in range(size)])


def merge(mine, theirs):
    top = jnp.maximum(mine[0:1], theirs[0:1])
    sums = mine * jnp.exp2(mine[0:1] - top) + theirs * jnp.exp2(theirs[0:1] - top)
    row = lax.broadcasted_iota(jnp.int32, mine.shape, 0)
    return jnp.where(row == 0, top, sums)


def log_add(one, two):
    return jnp.maximum(one, two) + jnp.log2(1.0 + jnp.exp2(-jnp.abs(one - two)))


def per_device(src_points, tgt_points, log_a, log_b, g_init):
    place = lax.axis_index("tgt")
    share = src_points.shape[1] // lax.axis_size("tgt")
    crossed = (place ^ (place >> 2) ^ (place >> 3)) & 1
    flag = crossed[None]
    with jax.named_scope("cross"):
        other_points = swap(src_points, 1, 0)
        other_a = swap(log_a, 1, 0)
    with jax.named_scope("gather_points_1"):
        more = swap(tgt_points, 1, Z_MASKS[0])
    with jax.named_scope("row_lse"):
        level = row_lse(flag, src_points, other_points, tgt_points, g_init[None, :])[0]
        more, level, other_a, tgt_mass, own_points = lax.optimization_barrier(
            (more, level, other_a, log_b, src_points)
        )
        near = jnp.concatenate([tgt_points, more], 1)
        src_mass = LOG2E * jnp.where(crossed == 1, other_a, log_a)
        tgt_mass = LOG2E * tgt_mass
        picks = [
            lax.dynamic_slice_in_dim(own_points, (place ^ k) * share, share, 1)
            for k in (0, 1, 3, 2)
        ]
        part = jnp.concatenate(picks, 1)
    with jax.named_scope("row_combine"):
        y2, y3 = swap(level, 0, 2), swap(level, 1, 3)
        y1 = swap(level, 1, 1)
        level = log_add(log_add(y2, y3), log_add(level, y1))
        for mask in T_MASKS:
            if mask == T_MASKS[-1]:
                near, level = lax.optimization_barrier((near, level))
            level = log_add(level, swap(level, 1, mask))
        src_term = src_mass - level
    with jax.named_scope("gather_points_2"):
        src_term, tgt_mass = lax.optimization_barrier((src_term, tgt_mass))
        more = swap(near, 1, Z_MASKS[1])
    with jax.named_scope("column_sums"):
        columns = weighted_sums(
            flag, [src_points, other_points], [src_term[None, :]], tgt_points
        )
        columns, more, level, own_points, own_targets = lax.optimization_barrier(
            (columns, more, level, src_points, tgt_points)
        )
        near = jnp.concatenate([near, more], 1)
    with jax.named_scope("column_combine"):
        columns = merge(columns, swap(columns, SRC_MASKS[0], 0))
        member = lax.axis_index("src")
        upper = (member ^ (member >> 1)) & 1 == 1
        columns = jnp.concatenate(
            [columns[0:8], jnp.where(upper, columns[16:24], columns[8:16])], 0
        )
        columns, near, level = lax.optimization_barrier((columns, near, level))
        for mask in SRC_MASKS[1:]:
            columns = merge(columns, swap(columns, mask, 0))
        tgt_term = tgt_mass - columns[0] - jnp.log2(columns[1])
    with jax.named_scope("gather_points_3"):
        second = lax.axis_index("src") & 1 == 1
        fetched = swap(jnp.where(second, near[8:16], near[0:8]), 1, Z_MASKS[2])
    with jax.named_scope("row_results"):
        level = jnp.where(crossed == 1, swap(level, 1, 0), level)
        f_new = ENTROPY * LN2 * (LOG2E * log_a - level) + jnp.sum(own_points * own_points, 0)

    with jax.named_scope("gather_term"):
        term = tgt_term[None, :]
        term = jnp.concatenate([term, swap(term, 1, Z_MASKS[0])], 1)
        kept = columns[8:16]
        other = swap(kept, 1, 0)
        term, tgt_term, other, fetched = lax.optimization_barrier((term, tgt_term, other, fetched))
        beside = swap(fetched, 1, 0)
        term = jnp.concatenate([term, swap(term, 1, Z_MASKS[1])], 1)
        far = jnp.concatenate(
            [jnp.where(second, fetched, beside), jnp.where(second, beside, fetched)], 0
        )
        term, far = lax.optimization_barrier((term, far))
        far_term = swap(term, 1, Z_MASKS[2])
    with jax.named_scope("column_results"):
        g_new = ENTROPY * LN2 * tgt_term + jnp.sum(own_targets * own_targets, 0)
        mass = jnp.concatenate([jnp.where(upper, other, kept), jnp.where(upper, kept, other)], 0)
        tgt_map = mass / columns[1:2]
    with jax.named_scope("row_sums"):
        half = 2 * share
        rows = weighted_sums(flag, [near], [term], part[:, half:])
        rows, far = lax.optimization_barrier((rows, far))
    with jax.named_scope("map_combine"):
        away = merge(rows, weighted_sums(flag, [far], [far_term], part[:, half:]))
        away, far_term = lax.optimization_barrier((away, far_term))
        away = swap(away, 0, 3)
        side = weighted_sums(flag, [near, far], [term, far_term], part[:, share:half])
        side = merge(away[:, share:], side)
        side, far_term = lax.optimization_barrier((side, far_term))
        side = swap(side, 0, 1)
        mine = weighted_sums(flag, [near, far], [term, far_term], part[:, :share])
        rows = merge(merge(away[:, :share], side), mine)
        src_map = rows[8:24] / rows[1:2]
    return (f_new, g_new, src_map, tgt_map)


def solution(mesh):
    in_specs = (P(None, "src"), P(None, "tgt"), P("src"), P("tgt"), P("tgt"))
    out_specs = (P("src"), P("tgt"), P(None, ("src", "tgt")), P(None, "tgt"))
    return jax.shard_map(
        per_device, mesh=mesh, in_specs=in_specs, out_specs=out_specs, check_vma=False
    )
```
